128 devices in a mesh: arc: 8 (over x_hi, z), col: 16 (over x_lo, y, core).
Axes of the slice: x: 4 (x_hi: 2, x_lo: 2; x = x_hi * 2 + x_lo), y: 4, z: 4, core: 2. Of those that a mesh axis runs over, the one named last changes fastest.
Arguments:
- local_obs: float32 [1024, 320, 128], P(('arc', 'col')), may hold values from -6 to 6
- global_obs: float32 [1024, 320, 512], P('arc', None, 'col'), may hold values from -0.75 to 0.75
- row_counts: int32 [1024], P('arc'), may hold values from 160 to 320, as said below
- owner_map: int32 [1024], P(('arc', 'col')), may hold values from 0 to 255, as said below
- prior_factor: float32 [256, 512, 512], P(('arc', 'col')), as said below
Outputs:
- updated_factor: float32 [256, 512, 512], P(('arc', 'col'))
The draws below stay inside these ranges and needn't reach their ends.
Inputs may be any that keep to these rules, and one draw needn't show every extreme that they name: `row_counts`: between 160 and 320; some arc has exactly 320 rows and another exactly 160. `owner_map`: the slice of arc k lies on a device with the same col index as the device that holds local_obs[k]; slice s lies on device s // 2 in arc+col order; from the 8 arcs of one device at most 2 have slices on devices of one arc index, and exactly 2 on one of them; in each col index one device receives 2 arcs from every device of that col index. `prior_factor`: each slice's factor is upper triangular with a positive diagonal.
All inputs are finite; a program needn't handle non-finite values.
Results may differ from the reference program's by a relative error of at most 0.0003.
Values sent between devices are 32-bit elements; how exact they have to be, the bound alone decides.
No kernel may reach another device: no remote copies, remote signals or barrier semaphores. Data moves between devices by JAX's collectives and lax.ppermute only.
A program may use at most 128 MiB of HBM per device.

```python
import jax
import jax.numpy as jnp
from jax import lax

LOC = 128
W = 512
ROWS = 320
SLICE_DEV = 2
ARC_DEV = 8
ARCS = 1024
NSLICE = 256
N_ARC = 8
N_COL = 16


def draw_row_counts(key, part):
    key = jax.random.fold_in(key, 7)
    key_base, key_first, key_second = jax.random.split(key, 3)
    counts = jax.random.randint(key_base, (ARCS,), ROWS // 2, ROWS + 1)
    first_pick = jax.random.randint(key_first, (), 0, ARCS)
    second_step = jax.random.randint(key_second, (), 1, ARCS)
    second_pick = (first_pick + second_step) % ARCS
    counts = counts.at[first_pick].set(ROWS).at[second_pick].set(ROWS // 2)
    return counts.astype(jnp.int32)


def draw_owner_map(key, part):
    key = jax.random.fold_in(key, 11)
    key_hot, key_other, key_order, key_slice = jax.random.split(key, 4)
    capacity = max(2, ARC_DEV // 4)
    device_total = N_ARC * N_COL
    hot_arc = jax.random.randint(key_hot, (N_COL,), 0, N_ARC)
    devices = jnp.arange(device_total, dtype=jnp.int32)
    col_index = devices % N_COL
    hot_dest = hot_arc[col_index]
    spare = (N_ARC - 1) * capacity
    other_keys = jax.random.split(key_other, device_total)
    picks = jax.vmap(lambda sub_key: jax.random.permutation(sub_key, spare))(other_keys)[:, :ARC_DEV - capacity]
    rank_other = (picks // capacity).astype(jnp.int32)
    other_dest = rank_other + (rank_other >= hot_dest[:, None]).astype(jnp.int32)
    hot_block = jnp.broadcast_to(hot_dest[:, None], (device_total, capacity)).astype(jnp.int32)
    dest_arc = jnp.concatenate([hot_block, other_dest], axis=1)
    order_keys = jax.random.split(key_order, device_total)
    shuffled = jax.vmap(lambda sub_key, dest_row: jax.random.permutation(sub_key, dest_row))(order_keys, dest_arc)
    slice_pick = jax.random.randint(key_slice, (device_total, ARC_DEV), 0, SLICE_DEV)
    owner = (shuffled * N_COL + col_index[:, None]) * SLICE_DEV + slice_pick
    return owner.reshape(-1).astype(jnp.int32)


def draw_prior_factor(key, part):
    key = jax.random.fold_in(key, 5)
    key_diag, key_upper = jax.random.split(key)
    diagonal = jax.random.uniform(key_diag, (NSLICE, W), minval=1.5, maxval=3.0)
    upper = jax.random.normal(key_upper, (NSLICE, W, W)) * (0.7 / W ** 0.5)
    places = jnp.arange(W)
    strict = (places[None, :] > places[:, None]).astype(jnp.float32)
    identity = (places[None, :] == places[:, None]).astype(jnp.float32)
    factor = upper * strict[None] + diagonal[:, :, None] * identity[None]
    return factor.astype(jnp.float32)


def shard_levels(rng, extent, cuts, low, high):
    level, own = 1.0, jax.random.fold_in(rng, 6)
    for axis_at, blocks in cuts:
        heights = jnp.exp(jax.random.uniform(jax.random.fold_in(own, axis_at), (blocks,), jnp.float32, low / len(cuts), high / len(cuts)))
        level = level * jnp.repeat(heights, extent[axis_at] // blocks).reshape([-1 if axis == axis_at else 1 for axis in range(len(extent))])
    return level


def bell_draw(stream_key, extent, scale, bound, pieces=(), held_as=jnp.bfloat16):
    loudness = shard_levels(stream_key, extent, pieces, -0.22, 0.18) if pieces else 1.0
    entries = jax.random.normal(stream_key, extent, jnp.float32) * scale * loudness
    return jnp.minimum(jnp.maximum(entries, -bound), bound).astype(held_as)


def setup_inputs(seed: int = 0) -> dict:
    keys = jax.random.split(jax.random.key(seed), 6)
    return {
        "local_obs": bell_draw(keys[0], (ARCS, ROWS, LOC), 1.0, 6.0, ((0, 128),), jnp.float32),
        "global_obs": bell_draw(keys[1], (ARCS, ROWS, W), 0.125, 0.75, ((0, 8), (2, 16)), jnp.float32),
        "row_counts": draw_row_counts(jax.random.fold_in(keys[5], 71), 0),
        "owner_map": draw_owner_map(jax.random.fold_in(keys[5], 71), 0),
        "prior_factor": draw_prior_factor(jax.random.fold_in(keys[5], 71), 0),
    }


highest_precision = lax.Precision.HIGHEST

def valid_row_mask(counts, maximum_row_count):
    places = lax.broadcasted_iota(jnp.int32, (counts.shape[0], maximum_row_count, 1), 1)
    return (places < counts[:, None, None]).astype(jnp.float32)

def orthonormal(local_part, weight_valid_mask):
    masked = local_part * weight_valid_mask
    local_gram = jnp.einsum('arl,arm->alm', masked, masked, precision=highest_precision)
    factor_low = jnp.linalg.cholesky(local_gram)
    return lax.linalg.triangular_solve(factor_low, masked, left_side=False, lower=True, transpose_a=True)

def eliminate_local_block(basis_vectors, global_block):
    coupling = jnp.einsum('arl,arc->alc', basis_vectors, global_block, precision=highest_precision)
    return global_block - jnp.einsum('arl,alc->arc', basis_vectors, coupling, precision=highest_precision)

def reference(local_obs, global_obs, row_counts, owner_map, prior_factor):
    maximum_row_count = local_obs.shape[1]
    information = jnp.einsum('sij,sik->sjk', prior_factor, prior_factor, precision=highest_precision)

    def add_arc(information, arc_item):
        local_part, global_block, arc_count, owner_slice = arc_item
        counts = arc_count[None]
        weight_valid_mask = valid_row_mask(counts, maximum_row_count)
        basis_vectors = orthonormal(local_part[None], weight_valid_mask)
        remaining_block = eliminate_local_block(basis_vectors, global_block[None] * weight_valid_mask)[0]
        matrix_product = jnp.dot(remaining_block.T, remaining_block, precision=highest_precision)
        current = lax.dynamic_index_in_dim(information, owner_slice, 0, keepdims=False)
        information = lax.dynamic_update_index_in_dim(information, current + matrix_product, owner_slice, 0)
        return (information, None)
    information, unused = lax.scan(add_arc, information, (local_obs, global_obs, row_counts, owner_map))
    factor_low = jnp.linalg.cholesky(information)
    return jnp.swapaxes(factor_low, 1, 2)
```

```python
import functools

import jax
import jax.numpy as jnp
from jax import lax
from jax.experimental import pallas as pl
from jax.experimental.pallas import tpu as pltpu
from jax.sharding import PartitionSpec as P

SLICE_DEV = 2
CHUNKS = 2
HI = lax.Precision.HIGHEST
F32 = jnp.float32
BF16 = jnp.bfloat16
NN = (((1,), (0,)), ((), ()))
NT = (((1,), (1,)), ((), ()))
TN = (((0,), (0,)), ((), ()))
VMEM_LIMIT = 48 * 1024 * 1024


def dot(a, b, dims, precision=None):
    return lax.dot_general(a, b, dims, precision=precision, preferred_element_type=F32)


def split2(x):
    high = x.astype(BF16)
    return high, (x - high.astype(F32)).astype(BF16)


def dot3(a, b, dims):
    ah, al = a
    bh, bl = b
    return dot(ah, bh, dims) + (dot(ah, bl, dims) + dot(al, bh, dims))


def split3(x):
    high = x.astype(BF16).astype(F32)
    rest = x - high
    mid = rest.astype(BF16).astype(F32)
    return high, mid, rest - mid


def outer6(left, right):
    lh, lm, ll = split3(left)
    rh, rm, rl = split3(right)
    a = jnp.concatenate([lh, lh, lm, lh, ll, lm], axis=0).astype(BF16)
    b = jnp.concatenate([rh, rm, rh, rl, rh, rm], axis=0).astype(BF16)
    return dot(a, b, TN)


def row_of(x, i):
    return jnp.broadcast_to(x[i : i + 1, :], x.shape)


def lane_of(x, i):
    return jnp.broadcast_to(x[:, i : i + 1], x.shape)


def panel_places(p):
    lane = lax.broadcasted_iota(jnp.int32, (8, 128), 1) - 8 * p
    sub = lax.broadcasted_iota(jnp.int32, (8, 128), 0)
    return lane, sub


def cholesky_panel(a_ref, b, p, store_upper):
    lane, sub = panel_places(p)
    x = a_ref[b, pl.ds(pl.multiple_of(8 * p, 8), 8), :]
    d = pltpu.roll(x, lax.rem(128 - 8 * p, 128), 1)
    c = [lane_of(d, l) for l in range(8)]
    m = [(sub == k).astype(F32) for k in range(8)]
    for i in range(8):
        r = lax.rsqrt(row_of(c[i], i))
        unit = (sub == i).astype(F32)
        lm = jnp.where(sub >= i, c[i] * r, 0.0) - unit
        for l in range(i + 1, 8):
            c[l] = c[l] - lm * (row_of(c[l], i) * r)
        for k in range(i + 1):
            m[k] = m[k] - lm * (row_of(m[k], i) * r)
    own = lane == sub
    inside = (lane >= 0) & (lane < 8)
    upper = m[0] * row_of(x, 0)
    for k in range(1, 8):
        upper = upper + m[k] * row_of(x, k)
    place = jnp.where(lane == 0, m[0], upper)
    for k in range(1, 8):
        place = jnp.where(lane == k, m[k], place)
    if store_upper is not None:
        store_upper(jnp.where(lane >= sub, upper, 0.0))
    t = outer6(jnp.where(lane >= 8, upper, 0.0), place)
    rows = lax.broadcasted_iota(jnp.int32, (128, 128), 0)
    lanes = lax.broadcasted_iota(jnp.int32, (128, 128), 1) - 8 * p
    cleared = (lanes >= 0) & (lanes < 8) & (rows >= 8 * p + 8)
    a_ref[b] = jnp.where(cleared, 0.0, a_ref[b]) - t
    a_ref[b, pl.ds(pl.multiple_of(8 * p, 8), 8), :] = place


def inverse_panel(a_ref, sign_ref, b, p):
    lane, sub = panel_places(p)
    x = a_ref[b, pl.ds(pl.multiple_of(8 * p, 8), 8), :]
    d = pltpu.roll(x, lax.rem(128 - 8 * p, 128), 1)
    c = [lane_of(d, l) for l in range(8)]
    m = [(sub == k).astype(F32) for k in range(8)]
    signs = sign_ref[b]
    for i in range(8):
        pv = row_of(c[i], i)
        s = jnp.where(pv >= 0.0, -1.0, 1.0)
        signs = jnp.where(lane == i, s, signs)
        inv = 1.0 / (pv - s)
        lm = jnp.where(sub == i, 1.0 - inv, c[i] * inv)
        for l in range(i + 1, 8):
            c[l] = c[l] - lm * row_of(c[l], i)
        for k in range(i + 1):
            m[k] = m[k] - lm * row_of(m[k], i)
    sign_ref[b] = signs
    place = m[0] * row_of(x, 0)
    for k in range(1, 8):
        place = place + m[k] * row_of(x, k)
    for k in range(8):
        place = jnp.where(lane == k, m[k], place)
    rows = lax.broadcasted_iota(jnp.int32, (128, 128), 0) - 8 * p
    lanes = lax.broadcasted_iota(jnp.int32, (128, 128), 1) - 8 * p
    wide = jnp.concatenate([place] * 16, axis=0)
    factor = jnp.where((rows >= 0) & (rows < 8), wide, 0.0)
    a = a_ref[b]
    t = dot(a, factor, NN, HI)
    a_ref[b] = jnp.where((lanes >= 0) & (lanes < 8), 0.0, a) - t
    a_ref[b, pl.ds(pl.multiple_of(8 * p, 8), 8), :] = place


def layout_kernel(x_ref, o_ref):
    rows, cols, arcs = x_ref.shape
    half = cols // 2
    for j in range(half):
        first = x_ref[:, j, :]
        second = x_ref[:, j + half, :]
        for tile in range(2):
            o_ref[:, tile * cols + j, :] = first[tile * 128 : tile * 128 + 128].T
            o_ref[:, tile * cols + j + half, :] = second[tile * 128 : tile * 128 + 128].T
        o_ref[:, 2 * cols + j, :] = jnp.concatenate([first[256:], second[256:]], axis=0).T


def layout(x, chunk):
    rows, cols, arcs = x.shape
    part = cols // CHUNKS
    packed = 2 * part + part // 2
    return pl.pallas_call(
        layout_kernel,
        out_shape=jax.ShapeDtypeStruct((arcs, packed, 128), F32),
        grid=(1,),
        in_specs=[pl.BlockSpec((rows, part, arcs), lambda i: (0, chunk, 0))],
        out_specs=pl.BlockSpec((arcs, packed, 128), lambda i: (0, 0, 0)),
        compiler_params=pltpu.CompilerParams(vmem_limit_bytes=VMEM_LIMIT),
    )(x)


def local_kernel(counts_ref, l_ref, z_ref, a_ref, q_ref, sign_ref):
    arcs, rows, loc = l_ref.shape
    place = lax.broadcasted_iota(jnp.int32, (rows, loc), 0)
    for b in range(arcs):
        masked = jnp.where(place < counts_ref[b], l_ref[b], 0.0)
        q_ref[b] = masked
        a_ref[b] = dot(masked, masked, TN, HI)

    def factor(p, carry):
        for b in range(arcs):
            cholesky_panel(a_ref, b, p, None)
        return carry

    lax.fori_loop(0, loc // 8, factor, 0)
    r = lax.broadcasted_iota(jnp.int32, (loc, loc), 0)
    l = lax.broadcasted_iota(jnp.int32, (loc, loc), 1)
    for b in range(arcs):
        basis = dot(q_ref[b], jnp.where(l <= r, a_ref[b], 0.0), NT, HI)
        q_ref[b] = basis
        a_ref[b] = basis[:loc]
    sign_ref[...] = jnp.zeros_like(sign_ref)

    def invert(p, carry):
        for b in range(arcs):
            inverse_panel(a_ref, sign_ref, b, p)
        return carry

    lax.fori_loop(0, loc // 8, invert, 0)
    rest = rows - loc
    unit = (place == lax.broadcasted_iota(jnp.int32, (rows, loc), 1)).astype(F32)
    r2 = lax.broadcasted_iota(jnp.int32, (rest, rows), 0)
    l2 = lax.broadcasted_iota(jnp.int32, (rest, rows), 1)
    for b in range(arcs):
        q = q_ref[b]
        n = dot(q[loc:], a_ref[b], NN, HI)
        v = q * sign_ref[b][0:1] - unit
        keep = (l2 == r2 + loc) & (l2 < counts_ref[b])
        z = dot(n, v, NT, HI) + keep.astype(F32)
        tail = z[:, 256:]
        gap = jnp.zeros_like(tail)
        wide = jnp.concatenate([z[:, :256], tail, gap, gap, tail], axis=1)
        blank = jnp.zeros((64, wide.shape[1]), F32)
        tall = jnp.concatenate([wide[:loc], blank, wide[loc:], blank], axis=0)
        zh, zl = split2(tall)
        z_ref[b, 0] = zh
        z_ref[b, 1] = zl


def local_part(counts, local_obs):
    arcs, rows, loc = local_obs.shape
    return pl.pallas_call(
        local_kernel,
        out_shape=jax.ShapeDtypeStruct((arcs, 2, rows, 512), BF16),
        in_specs=[pl.BlockSpec(memory_space=pltpu.SMEM), pl.BlockSpec(memory_space=pltpu.VMEM)],
        out_specs=pl.BlockSpec(memory_space=pltpu.VMEM),
        scratch_shapes=[
            pltpu.VMEM((arcs, loc, loc), F32),
            pltpu.VMEM((arcs, rows, loc), F32),
            pltpu.VMEM((arcs, 8, loc), F32),
        ],
        compiler_params=pltpu.CompilerParams(vmem_limit_bytes=VMEM_LIMIT),
    )(counts, local_obs)


def eliminate_kernel(dest_ref, slot_ref, g_ref, z_ref, o_ref):
    sources, arcs, packed, _ = g_ref.shape
    part = packed * 2 // 5
    half = part // 2
    width = sources * part
    o_ref[...] = jnp.zeros_like(o_ref)

    def arc(a, carry):
        slot = slot_ref[a]
        dest = dest_ref[a]
        tails = pl.ds(pl.multiple_of(192 - 64 * slot, 64), 128)
        z = [jnp.concatenate([z_ref[a, i, :128, :], z_ref[a, i, tails, :]], axis=0) for i in range(2)]
        g = [g_ref[:, a, i * part : (i + 1) * part, :].reshape(width, 128) for i in range(2)]
        t = split2(g_ref[:, a, 2 * part :, :].reshape(width // 2, 128))
        body = dot3(split2(jnp.concatenate(g, axis=1)), [w[:, :256] for w in z], NT)
        ends = [dot3(t, [w[:, 256 + 128 * i : 384 + 128 * i] for w in z], NT) for i in range(2)]
        ends = jnp.stack([e.reshape(sources, half, 256) for e in ends], axis=1).reshape(width, 256)
        r = body + ends
        o_ref[dest, :, pl.ds(pl.multiple_of(256 * slot, 128), 128)] = r[:, :128]
        o_ref[dest, :, 128:256] = o_ref[dest, :, 128:256] + r[:, 128:]
        return carry

    lax.fori_loop(0, arcs, arc, 0)


def eliminate(dest, slot, g, z, groups):
    sources, arcs, packed, _ = g.shape
    width = sources * packed * 2 // 5
    smem = pl.BlockSpec(memory_space=pltpu.SMEM)
    vmem = pl.BlockSpec(memory_space=pltpu.VMEM)
    return pl.pallas_call(
        eliminate_kernel,
        out_shape=jax.ShapeDtypeStruct((groups, width, 384), F32),
        in_specs=[smem, smem, vmem, vmem],
        out_specs=vmem,
        compiler_params=pltpu.CompilerParams(vmem_limit_bytes=VMEM_LIMIT),
    )(dest, slot, g, z)


def factor_kernel(part, labels_ref, *refs):
    arrived = refs[:CHUNKS]
    prior_ref, out_ref, info_ref, high_ref, low_ref, a_ref = refs[CHUNKS:]
    slices, width, _ = prior_ref.shape
    groups = arrived[0].shape[0]
    half = width // 2
    info_ref[...] = prior_ref[...]
    lane = lax.broadcasted_iota(jnp.int32, (width, 384), 1)

    def add(n, carry):
        first, second = labels_ref[2 * n], labels_ref[2 * n + 1]
        pieces = [a[n].reshape(width // (CHUNKS * part), 1, part, 384) for a in arrived]
        x = jnp.concatenate(pieces, axis=1).reshape(width, 384)
        xh, xl = split2(x)
        high_ref[...] = xh
        low_ref[...] = xl
        for s in range(slices):

            @pl.when((first == s) | (second == s))
            def _():
                own = jnp.where(lane < 192, first, second) == s
                h, l = high_ref[...], low_ref[...]
                mh = jnp.where(own, h, jnp.zeros_like(h))
                ml = jnp.where(own, l, jnp.zeros_like(l))
                info_ref[s, :half] += dot3((mh[:half], ml[:half]), (h, l), NT)
                info_ref[s, half:, half:] += dot3((mh[half:], ml[half:]), (h[half:], l[half:]), NT)

        return carry

    lax.fori_loop(0, groups, add, 0)
    r = lax.broadcasted_iota(jnp.int32, (128, 128), 0)
    l = lax.broadcasted_iota(jnp.int32, (128, 128), 1)
    for k in range(width // 128):
        lo, hi = 128 * k, 128 * k + 128
        for s in range(slices):
            a_ref[s] = info_ref[s, lo:hi, lo:hi]
            if k:
                out_ref[s, lo:hi, :lo] = jnp.zeros((128, lo), F32)

        def step(p, carry):
            for s in range(slices):

                def store(rows):
                    out_ref[s, pl.ds(pl.multiple_of(lo + 8 * p, 8), 8), lo:hi] = rows

                cholesky_panel(a_ref, s, p, store)
            return carry

        lax.fori_loop(0, 16, step, 0)
        if hi < width:
            for s in range(slices):
                inverse = jnp.where(l <= r, a_ref[s], 0.0)
                u = dot(inverse, info_ref[s, lo:hi, hi:], NN, HI)
                out_ref[s, lo:hi, hi:] = u
                for j in range(hi, width, 128):
                    info_ref[s, j : j + 128, j:] -= dot(u[:, j - hi : j - hi + 128], u[:, j - hi :], TN, HI)


def factor(part, labels, arrived, prior_gram):
    slices, width, _ = prior_gram.shape
    vmem = pl.BlockSpec(memory_space=pltpu.VMEM)
    return pl.pallas_call(
        functools.partial(factor_kernel, part),
        out_shape=jax.ShapeDtypeStruct(prior_gram.shape, F32),
        in_specs=[pl.BlockSpec(memory_space=pltpu.SMEM)] + [vmem] * (CHUNKS + 1),
        out_specs=vmem,
        scratch_shapes=[
            pltpu.VMEM((slices, width, width), F32),
            pltpu.VMEM((width, 384), BF16),
            pltpu.VMEM((width, 384), BF16),
            pltpu.VMEM((slices, 128, 128), F32),
        ],
        compiler_params=pltpu.CompilerParams(vmem_limit_bytes=VMEM_LIMIT),
    )(labels, *arrived, prior_gram)


def slots_of(owner, col_groups):
    dest = owner // SLICE_DEV // col_groups
    order = jnp.arange(owner.shape[-1], dtype=jnp.int32)
    earlier = (dest[..., None, :] == dest[..., :, None]) & (order[None, :] < order[:, None])
    return dest, jnp.sum(earlier.astype(jnp.int32), axis=-1), owner % SLICE_DEV


def per_device(local_obs, global_obs, row_counts, owner_map, prior_factor):
    arc_dev = local_obs.shape[0]
    arc_groups = lax.axis_size("arc")
    col_groups = lax.axis_size("col")
    part = global_obs.shape[2] // CHUNKS
    counts = lax.dynamic_slice_in_dim(row_counts, lax.axis_index("col") * arc_dev, arc_dev)
    x = jnp.transpose(global_obs, (1, 2, 0))
    columns = []
    for h in range(CHUNKS):
        packed = layout(x, h)
        moved = lax.all_to_all(packed, "col", split_axis=0, concat_axis=0, tiled=True)
        columns.append(moved.reshape(col_groups, arc_dev, *moved.shape[1:]))
    owners = lax.all_gather(owner_map, "arc", axis=0)
    dest, slot, label = slots_of(owners, col_groups)
    mine = (dest == lax.axis_index("arc"))[:, :, None] & (slot[:, :, None] == jnp.arange(2, dtype=jnp.int32))
    labels = (jnp.sum(jnp.where(mine, label[:, :, None] + 1, 0), axis=1) - 1).reshape(-1)
    own_dest, own_slot, _ = slots_of(owner_map, col_groups)
    z = local_part(counts, local_obs)
    prior_gram = jnp.einsum("sij,sik->sjk", prior_factor, prior_factor, precision=HI)
    arrived = []
    for h in range(CHUNKS):
        kept = eliminate(own_dest, own_slot, columns[h], z, arc_groups)
        arrived.append(lax.all_to_all(kept, "arc", split_axis=0, concat_axis=0, tiled=True))
    return factor(part, labels, arrived, prior_gram)


def solution(mesh):
    placed = (
        P(("arc", "col"), None, None),
        P("arc", None, "col"),
        P("arc"),
        P(("arc", "col")),
        P(("arc", "col"), None, None),
    )
    return jax.shard_map(
        per_device,
        mesh=mesh,
        in_specs=placed,
        out_specs=P(("arc", "col"), None, None),
        check_vma=False,
    )
```

```python
import functools

import jax
import jax.numpy as jnp
from jax import lax
from jax.experimental import pallas as pl
from jax.experimental.pallas import tpu as pltpu
from jax.sharding import PartitionSpec as P

SLICE_DEV = 2
CHUNKS = 1
GROUP = 8
HI = lax.Precision.HIGHEST
F32 = jnp.float32
BF16 = jnp.bfloat16
NN = (((1,), (0,)), ((), ()))
NT = (((1,), (1,)), ((), ()))
TN = (((0,), (0,)), ((), ()))
VMEM_LIMIT = 48 * 1024 * 1024


def dot(a, b, dims, precision=None):
    return lax.dot_general(a, b, dims, precision=precision, preferred_element_type=F32)


def split2(x):
    high = x.astype(BF16)
    return high, (x - high.astype(F32)).astype(BF16)


def dot3(a, b, dims):
    ah, al = a
    bh, bl = b
    return dot(ah, bh, dims) + (dot(ah, bl, dims) + dot(al, bh, dims))


def split3(x):
    high = x.astype(BF16).astype(F32)
    rest = x - high
    mid = rest.astype(BF16).astype(F32)
    return high, mid, rest - mid


def outer6(left, right):
    lh, lm, ll = split3(left)
    rh, rm, rl = split3(right)
    a = jnp.concatenate([lh, lh, lm, lh, ll, lm], axis=0).astype(BF16)
    b = jnp.concatenate([rh, rm, rh, rl, rh, rm], axis=0).astype(BF16)
    return dot(a, b, TN)


def row_of(x, i):
    return jnp.broadcast_to(x[:, i : i + 1, :], x.shape)


def lane_of(x, i):
    return jnp.broadcast_to(x[:, :, i : i + 1], x.shape)


def panel_of(a_ref, which, p):
    rows = pl.ds(pl.multiple_of(8 * p, 8), 8)
    x = a_ref[which, rows, :]
    lane = lax.broadcasted_iota(jnp.int32, x.shape, 2) - 8 * p
    sub = lax.broadcasted_iota(jnp.int32, x.shape, 1)
    turned = pltpu.roll(x, lax.rem(128 - 8 * p, 128), 2)
    c = [lane_of(turned, l) for l in range(8)]
    m = [(sub == k).astype(F32) for k in range(8)]
    return rows, x, lane, sub, c, m


def apply_panel(m, x):
    terms = [m[k] * row_of(x, k) for k in range(8)]
    while len(terms) > 1:
        terms = [terms[i] + terms[i + 1] for i in range(0, len(terms), 2)]
    return terms[0]


def cholesky_panel(a_ref, which, p, store_upper):
    rows, x, lane, sub, c, m = panel_of(a_ref, which, p)
    for i in range(8):
        r = lax.rsqrt(row_of(c[i], i))
        lm = jnp.where(sub >= i, c[i] * r, 0.0) - (sub == i).astype(F32)
        for l in range(i + 1, 8):
            c[l] = c[l] - lm * (row_of(c[l], i) * r)
        for k in range(i + 1):
            m[k] = m[k] - lm * (row_of(m[k], i) * r)
    upper = apply_panel(m, x)
    place = upper
    for k in range(8):
        place = jnp.where(lane == k, m[k], place)
    if store_upper is not None:
        store_upper(jnp.where(lane >= sub, upper, 0.0))
    left = jnp.where(lane >= 8, upper, 0.0)
    t = jnp.stack([outer6(left[b], place[b]) for b in range(x.shape[0])], axis=0)
    a = a_ref[which]
    at_row = lax.broadcasted_iota(jnp.int32, a.shape, 1)
    at_lane = lax.broadcasted_iota(jnp.int32, a.shape, 2) - 8 * p
    cleared = (at_lane >= 0) & (at_lane < 8) & (at_row >= 8 * p + 8)
    a_ref[which] = jnp.where(cleared, 0.0, a) - t
    a_ref[which, rows, :] = place


def inverse_panel(a_ref, sign_ref, which, p):
    rows, x, lane, sub, c, m = panel_of(a_ref, which, p)
    signs = sign_ref[which]
    for i in range(8):
        pv = row_of(c[i], i)
        s = jnp.where(pv >= 0.0, -1.0, 1.0)
        signs = jnp.where(lane == i, s, signs)
        inv = 1.0 / (pv - s)
        lm = jnp.where(sub == i, 1.0 - inv, c[i] * inv)
        for l in range(i + 1, 8):
            c[l] = c[l] - lm * row_of(c[l], i)
        for k in range(i + 1):
            m[k] = m[k] - lm * row_of(m[k], i)
    sign_ref[which] = signs
    place = apply_panel(m, x)
    for k in range(8):
        place = jnp.where(lane == k, m[k], place)
    a = a_ref[which]
    at_row = lax.broadcasted_iota(jnp.int32, a.shape, 1) - 8 * p
    at_lane = lax.broadcasted_iota(jnp.int32, a.shape, 2) - 8 * p
    wide = jnp.concatenate([place] * 16, axis=1)
    factor = jnp.where((at_row >= 0) & (at_row < 8), wide, 0.0)
    t = jnp.stack([dot(a[b], factor[b], NN, HI) for b in range(x.shape[0])], axis=0)
    a_ref[which] = jnp.where((at_lane >= 0) & (at_lane < 8), 0.0, a) - t
    a_ref[which, rows, :] = place


def layout_kernel(x_ref, o_ref):
    rows, cols, arcs = x_ref.shape
    half = cols // 2
    for j in range(half):
        first = x_ref[:, j, :]
        second = x_ref[:, j + half, :]
        for tile in range(2):
            o_ref[:, tile * cols + j, :] = first[tile * 128 : tile * 128 + 128].T
            o_ref[:, tile * cols + j + half, :] = second[tile * 128 : tile * 128 + 128].T
        o_ref[:, 2 * cols + j, :] = jnp.concatenate([first[256:], second[256:]], axis=0).T


def layout(x, chunk):
    rows, cols, arcs = x.shape
    part = cols // CHUNKS
    packed = 2 * part + part // 2
    return pl.pallas_call(
        layout_kernel,
        out_shape=jax.ShapeDtypeStruct((arcs, packed, 128), F32),
        grid=(1,),
        in_specs=[pl.BlockSpec((rows, part, arcs), lambda i: (0, chunk, 0))],
        out_specs=pl.BlockSpec((arcs, packed, 128), lambda i: (0, 0, 0)),
        compiler_params=pltpu.CompilerParams(vmem_limit_bytes=VMEM_LIMIT),
    )(x)


def local_kernel(counts_ref, l_ref, z_ref, a_ref, q_ref, sign_ref):
    arcs, rows, loc = l_ref.shape
    place = lax.broadcasted_iota(jnp.int32, (rows, loc), 0)
    for b in range(arcs):
        masked = jnp.where(place < counts_ref[b], l_ref[b], 0.0)
        q_ref[b] = masked
        a_ref[b] = dot(masked, masked, TN, HI)

    def factor(p, carry):
        for b in range(0, arcs, GROUP):
            cholesky_panel(a_ref, slice(b, b + GROUP), p, None)
        return carry

    lax.fori_loop(0, loc // 8, factor, 0)
    r = lax.broadcasted_iota(jnp.int32, (loc, loc), 0)
    l = lax.broadcasted_iota(jnp.int32, (loc, loc), 1)
    for b in range(arcs):
        basis = dot(q_ref[b], jnp.where(l <= r, a_ref[b], 0.0), NT, HI)
        q_ref[b] = basis
        a_ref[b] = basis[:loc]
    sign_ref[...] = jnp.zeros_like(sign_ref)

    def invert(p, carry):
        for b in range(0, arcs, GROUP):
            inverse_panel(a_ref, sign_ref, slice(b, b + GROUP), p)
        return carry

    lax.fori_loop(0, loc // 8, invert, 0)
    rest = rows - loc
    unit = (place == lax.broadcasted_iota(jnp.int32, (rows, loc), 1)).astype(F32)
    r2 = lax.broadcasted_iota(jnp.int32, (rest, rows), 0)
    l2 = lax.broadcasted_iota(jnp.int32, (rest, rows), 1)
    for b in range(arcs):
        q = q_ref[b]
        n = dot(q[loc:], a_ref[b], NN, HI)
        v = q * sign_ref[b][0:1] - unit
        keep = (l2 == r2 + loc) & (l2 < counts_ref[b])
        z = dot(n, v, NT, HI) + keep.astype(F32)
        tail = z[:, 256:]
        gap = jnp.zeros_like(tail)
        wide = jnp.concatenate([z[:, :256], tail, gap, gap, tail], axis=1)
        blank = jnp.zeros((64, wide.shape[1]), F32)
        tall = jnp.concatenate([wide[:loc], blank, wide[loc:], blank], axis=0)
        zh, zl = split2(tall)
        z_ref[b, 0] = zh
        z_ref[b, 1] = zl


def local_part(counts, local_obs):
    arcs, rows, loc = local_obs.shape
    return pl.pallas_call(
        local_kernel,
        out_shape=jax.ShapeDtypeStruct((arcs, 2, rows, 512), BF16),
        in_specs=[pl.BlockSpec(memory_space=pltpu.SMEM), pl.BlockSpec(memory_space=pltpu.VMEM)],
        out_specs=pl.BlockSpec(memory_space=pltpu.VMEM),
        scratch_shapes=[
            pltpu.VMEM((arcs, loc, loc), F32),
            pltpu.VMEM((arcs, rows, loc), F32),
            pltpu.VMEM((arcs, 8, loc), F32),
        ],
        compiler_params=pltpu.CompilerParams(vmem_limit_bytes=VMEM_LIMIT),
    )(counts, local_obs)


def eliminate_kernel(dest_ref, slot_ref, g_ref, z_ref, o_ref):
    sources, arcs, packed, _ = g_ref.shape
    part = packed * 2 // 5
    half = part // 2
    width = sources * part
    o_ref[...] = jnp.zeros_like(o_ref)

    def arc(a, carry):
        slot = slot_ref[a]
        dest = dest_ref[a]
        tails = pl.ds(pl.multiple_of(192 - 64 * slot, 64), 128)
        z = [jnp.concatenate([z_ref[a, i, :128, :], z_ref[a, i, tails, :]], axis=0) for i in range(2)]
        g = [g_ref[:, a, i * part : (i + 1) * part, :].reshape(width, 128) for i in range(2)]
        t = split2(g_ref[:, a, 2 * part :, :].reshape(width // 2, 128))
        body = dot3(split2(jnp.concatenate(g, axis=1)), [w[:, :256] for w in z], NT)
        ends = [dot3(t, [w[:, 256 + 128 * i : 384 + 128 * i] for w in z], NT) for i in range(2)]
        ends = jnp.stack([e.reshape(sources, half, 256) for e in ends], axis=1).reshape(width, 256)
        r = body + ends
        o_ref[dest, :, pl.ds(pl.multiple_of(256 * slot, 128), 128)] = r[:, :128]
        o_ref[dest, :, 128:256] = o_ref[dest, :, 128:256] + r[:, 128:]
        return carry

    lax.fori_loop(0, arcs, arc, 0)


def eliminate(dest, slot, g, z, groups):
    sources, arcs, packed, _ = g.shape
    width = sources * packed * 2 // 5
    smem = pl.BlockSpec(memory_space=pltpu.SMEM)
    vmem = pl.BlockSpec(memory_space=pltpu.VMEM)
    return pl.pallas_call(
        eliminate_kernel,
        out_shape=jax.ShapeDtypeStruct((groups, width, 384), F32),
        in_specs=[smem, smem, vmem, vmem],
        out_specs=vmem,
        compiler_params=pltpu.CompilerParams(vmem_limit_bytes=VMEM_LIMIT),
    )(dest, slot, g, z)


def factor_kernel(part, labels_ref, *refs):
    arrived = refs[:CHUNKS]
    prior_ref, out_ref, info_ref, high_ref, low_ref, a_ref = refs[CHUNKS:]
    slices, width, _ = prior_ref.shape
    groups = arrived[0].shape[0]
    half = width // 2
    info_ref[...] = prior_ref[...]
    lane = lax.broadcasted_iota(jnp.int32, (width, 384), 1)

    def add(n, carry):
        first, second = labels_ref[2 * n], labels_ref[2 * n + 1]
        pieces = [a[n].reshape(width // (CHUNKS * part), 1, part, 384) for a in arrived]
        x = jnp.concatenate(pieces, axis=1).reshape(width, 384)
        xh, xl = split2(x)
        high_ref[...] = xh
        low_ref[...] = xl
        for s in range(slices):

            @pl.when((first == s) | (second == s))
            def _():
                own = jnp.where(lane < 192, first, second) == s
                h, l = high_ref[...], low_ref[...]
                mh = jnp.where(own, h, jnp.zeros_like(h))
                ml = jnp.where(own, l, jnp.zeros_like(l))
                info_ref[s, :half] += dot3((mh[:half], ml[:half]), (h, l), NT)
                info_ref[s, half:, half:] += dot3((mh[half:], ml[half:]), (h[half:], l[half:]), NT)

        return carry

    lax.fori_loop(0, groups, add, 0)
    r = lax.broadcasted_iota(jnp.int32, (128, 128), 0)
    l = lax.broadcasted_iota(jnp.int32, (128, 128), 1)
    for k in range(width // 128):
        lo, hi = 128 * k, 128 * k + 128
        for s in range(slices):
            a_ref[s] = info_ref[s, lo:hi, lo:hi]
            if k:
                out_ref[s, lo:hi, :lo] = jnp.zeros((128, lo), F32)

        def step(p, carry):
            def store(rows):
                out_ref[:, pl.ds(pl.multiple_of(lo + 8 * p, 8), 8), lo:hi] = rows

            cholesky_panel(a_ref, slice(0, slices), p, store)
            return carry

        lax.fori_loop(0, 16, step, 0)
        if hi < width:
            for s in range(slices):
                inverse = jnp.where(l <= r, a_ref[s], 0.0)
                u = dot(inverse, info_ref[s, lo:hi, hi:], NN, HI)
                out_ref[s, lo:hi, hi:] = u
                for j in range(hi, width, 128):
                    info_ref[s, j : j + 128, j:] -= dot(u[:, j - hi : j - hi + 128], u[:, j - hi :], TN, HI)


def factor(part, labels, arrived, prior_gram):
    slices, width, _ = prior_gram.shape
    vmem = pl.BlockSpec(memory_space=pltpu.VMEM)
    return pl.pallas_call(
        functools.partial(factor_kernel, part),
        out_shape=jax.ShapeDtypeStruct(prior_gram.shape, F32),
        in_specs=[pl.BlockSpec(memory_space=pltpu.SMEM)] + [vmem] * (CHUNKS + 1),
        out_specs=vmem,
        scratch_shapes=[
            pltpu.VMEM((slices, width, width), F32),
            pltpu.VMEM((width, 384), BF16),
            pltpu.VMEM((width, 384), BF16),
            pltpu.VMEM((slices, 128, 128), F32),
        ],
        compiler_params=pltpu.CompilerParams(vmem_limit_bytes=VMEM_LIMIT),
    )(labels, *arrived, prior_gram)


def slots_of(owner, col_groups):
    dest = owner // SLICE_DEV // col_groups
    order = jnp.arange(owner.shape[-1], dtype=jnp.int32)
    earlier = (dest[..., None, :] == dest[..., :, None]) & (order[None, :] < order[:, None])
    return dest, jnp.sum(earlier.astype(jnp.int32), axis=-1), owner % SLICE_DEV


def per_device(local_obs, global_obs, row_counts, owner_map, prior_factor):
    arc_dev = local_obs.shape[0]
    arc_groups = lax.axis_size("arc")
    col_groups = lax.axis_size("col")
    part = global_obs.shape[2] // CHUNKS
    counts = lax.dynamic_slice_in_dim(row_counts, lax.axis_index("col") * arc_dev, arc_dev)
    x = jnp.transpose(global_obs, (1, 2, 0))
    columns = []
    for h in range(CHUNKS):
        packed = layout(x, h)
        moved = lax.all_to_all(packed, "col", split_axis=0, concat_axis=0, tiled=True)
        columns.append(moved.reshape(col_groups, arc_dev, *moved.shape[1:]))
    owners = lax.all_gather(owner_map, "arc", axis=0)
    dest, slot, label = slots_of(owners, col_groups)
    mine = (dest == lax.axis_index("arc"))[:, :, None] & (slot[:, :, None] == jnp.arange(2, dtype=jnp.int32))
    labels = (jnp.sum(jnp.where(mine, label[:, :, None] + 1, 0), axis=1) - 1).reshape(-1)
    own_dest, own_slot, _ = slots_of(owner_map, col_groups)
    z = local_part(counts, local_obs)
    prior_gram = jnp.einsum("sij,sik->sjk", prior_factor, prior_factor, precision=HI)
    arrived = []
    for h in range(CHUNKS):
        kept = eliminate(own_dest, own_slot, columns[h], z, arc_groups)
        arrived.append(lax.all_to_all(kept, "arc", split_axis=0, concat_axis=0, tiled=True))
    return factor(part, labels, arrived, prior_gram)


def solution(mesh):
    placed = (
        P(("arc", "col"), None, None),
        P("arc", None, "col"),
        P("arc"),
        P(("arc", "col")),
        P(("arc", "col"), None, None),
    )
    return jax.shard_map(
        per_device,
        mesh=mesh,
        in_specs=placed,
        out_specs=P(("arc", "col"), None, None),
        check_vma=False,
    )
```

```python
import functools

import jax
import jax.numpy as jnp
from jax import lax
from jax.experimental import pallas as pl
from jax.experimental.pallas import tpu as pltpu
from jax.sharding import PartitionSpec as P

SLICE_DEV = 2
HI = lax.Precision.HIGHEST
F32 = jnp.float32
BF16 = jnp.bfloat16
NN = (((1,), (0,)), ((), ()))
NT = (((1,), (1,)), ((), ()))
TN = (((0,), (0,)), ((), ()))
VMEM_LIMIT = 48 * 1024 * 1024


def dot(a, b, dims, precision=None):
    return lax.dot_general(a, b, dims, precision=precision, preferred_element_type=F32)


def split2(x):
    high = x.astype(BF16)
    return high, (x - high.astype(F32)).astype(BF16)


def dot3(a, b, dims):
    ah, al = a
    bh, bl = b
    return dot(ah, bh, dims) + (dot(ah, bl, dims) + dot(al, bh, dims))


def split3(x):
    high = x.astype(BF16).astype(F32)
    rest = x - high
    mid = rest.astype(BF16).astype(F32)
    return high, mid, rest - mid


def outer6(left, right):
    lh, lm, ll = split3(left)
    rh, rm, rl = split3(right)
    a = jnp.concatenate([lh, lh, lm, lh, ll, lm], axis=0).astype(BF16)
    b = jnp.concatenate([rh, rm, rh, rl, rh, rm], axis=0).astype(BF16)
    return dot(a, b, TN)


def outer3(left, right):
    lh, lm, _ = split3(left)
    rh, rm, _ = split3(right)
    a = jnp.concatenate([lh, lh, left - lh], axis=0).astype(BF16)
    b = jnp.concatenate([rh, right - rh, rh], axis=0).astype(BF16)
    return dot(a, b, TN)


def row_of(x, i):
    return jnp.broadcast_to(x[:, i : i + 1, :], x.shape)


def lane_of(x, i):
    return jnp.broadcast_to(x[:, :, i : i + 1], x.shape)


def panel_rows(p):
    return pl.ds(pl.multiple_of(8 * p, 8), 8)


def places(x, p):
    lane = lax.broadcasted_iota(jnp.int32, x.shape, 2) - 8 * p
    return lane, lax.broadcasted_iota(jnp.int32, x.shape, 1)


def columns_of(x, p):
    turned = pltpu.roll(x, lax.rem(128 - 8 * p, 128), 2)
    return [lane_of(turned, l) for l in range(8)]


def batch_panel(x, following, p):
    lane, sub = places(x, p)
    inside = (lane >= 0) & (lane < 8)
    c = columns_of(x, p)
    n = columns_of(following, p)
    place = jnp.where(inside, (lane == sub).astype(F32), x)
    following = jnp.where(inside, 0.0, following)
    pivots = x
    for i in range(8):
        d = row_of(c[i], i)
        inv = pl.reciprocal(d, approx=True)
        pivots = jnp.where(sub == i, d, pivots)
        below = jnp.where(sub > i, c[i], 0.0)
        below_n = n[i]
        for l in range(i + 1, 8):
            r = row_of(c[l], i)
            c[l] = c[l] - (below * r) * inv
            n[l] = n[l] - (below_n * r) * inv
        below = below * inv
        r = row_of(place, i)
        place = place - below * r
        following = following - (below_n * inv) * r
    scale = lax.rsqrt(pivots)
    return place * scale, following


def cholesky_batch(a_ref):
    count = a_ref.shape[0]

    def step(p, carry):
        left, right, x = carry
        a = a_ref[...]
        at_lane, at_row = places(a, p)
        t = jnp.stack([outer6(left[b], right[b]) for b in range(count)], axis=0)
        cleared = (at_lane < 0) & (at_lane >= -8) & (at_row >= 8 * p + 8)
        a_ref[...] = jnp.where(cleared, 0.0, a) - t
        following = a_ref[:, panel_rows(jnp.minimum(p + 1, 15)), :]
        place, following = batch_panel(x, following, p)
        lane, sub = places(x, p)
        a_ref[:, panel_rows(p), :] = place
        return jnp.where(lane >= 16, place, 0.0), place, following

    first = a_ref[:, :8, :]
    lax.fori_loop(0, 16, step, (jnp.zeros_like(first), jnp.zeros_like(first), first))


def columns_at(x, p):
    return [lane_of(x, 8 * p + l) for l in range(8)]


def cholesky_panel(x, c, following, p):
    lane, sub = places(x, p)
    inside = (lane >= 0) & (lane < 8)
    c = list(c)
    place = jnp.where(inside, (lane == sub).astype(F32), x)
    n = ahead = None
    if following is not None:
        n = columns_at(following, p)
        ahead = columns_at(following, p + 1)
        following = jnp.where(inside, 0.0, following)
    upper = x
    pivots = x
    for i in range(8):
        d = row_of(c[i], i)
        inv = pl.reciprocal(d, approx=True)
        pivots = jnp.where(sub == i, d, pivots)
        below = jnp.where(sub > i, c[i], 0.0)
        for l in range(i + 1, 8):
            r = row_of(c[l], i) * inv
            c[l] = c[l] - below * r
            if n is not None:
                n[l] = n[l] - n[i] * r
        r = row_of(place, i) * inv
        place = place - below * r
        if n is not None:
            following = following - n[i] * r
            less = n[i] * inv
            ahead = [ahead[l] - less * row_of(n[i], l) for l in range(8)]
        upper = upper - below * (row_of(upper, i) * inv)
    scale = lax.rsqrt(pivots)
    return upper * scale, place * scale, following, ahead


def cholesky_blocks(a_ref, store_upper):
    count = a_ref.shape[0]
    rows = [a_ref[:, 8 * q : 8 * q + 8, :] for q in range(16)]
    c = columns_at(rows[0], 0)
    for p in range(16):
        following = rows[p + 1] if p < 15 else None
        upper, place, following, c = cholesky_panel(rows[p], c, following, p)
        lane, sub = places(place, p)
        inside = (lane >= 0) & (lane < 8)
        a_ref[:, 8 * p : 8 * p + 8, :] = place
        if store_upper is not None:
            store_upper(p, jnp.where(lane >= sub, upper, 0.0))
        if p < 15:
            rows[p + 1] = following
        if p < 14:
            left = jnp.where(lane >= 16, place, 0.0)
            t = [outer3(left[b], place[b]) for b in range(count)]
            for q in range(p + 2, 16):
                part = jnp.stack([v[8 * q : 8 * q + 8] for v in t], axis=0)
                rows[q] = jnp.where(inside, 0.0, rows[q]) - part


def inverse_panel(a_ref, sign_ref, p):
    x = a_ref[:, panel_rows(p), :]
    lane, sub = places(x, p)
    c = columns_of(x, p)
    place = jnp.where((lane >= 0) & (lane < 8), (lane == sub).astype(F32), x)
    signs = sign_ref[...]
    for i in range(8):
        pv = row_of(c[i], i)
        s = jnp.where(pv >= 0.0, -1.0, 1.0)
        signs = jnp.where(lane == i, s, signs)
        inv = pl.reciprocal(pv - s, approx=True)
        lm = jnp.where(sub == i, 1.0 - inv, c[i] * inv)
        for l in range(i + 1, 8):
            c[l] = c[l] - lm * row_of(c[l], i)
        place = place - lm * row_of(place, i)
    sign_ref[...] = signs
    a = a_ref[...]
    at_lane, at_row = places(a, p)
    wide = jnp.concatenate([place] * 16, axis=1)
    factor = jnp.where((at_row >= 8 * p) & (at_row < 8 * p + 8), wide, 0.0)
    t = jnp.stack([dot(a[b], factor[b], NN, HI) for b in range(x.shape[0])], axis=0)
    a_ref[...] = jnp.where((at_lane >= 0) & (at_lane < 8), 0.0, a) - t
    a_ref[:, panel_rows(p), :] = place


def layout_kernel(x_ref, o_ref):
    rows, cols, arcs = x_ref.shape
    half = cols // 2
    for j in range(half):
        first = x_ref[:, j, :]
        second = x_ref[:, j + half, :]
        for tile in range(2):
            o_ref[:, tile * cols + j, :] = first[tile * 128 : tile * 128 + 128].T
            o_ref[:, tile * cols + j + half, :] = second[tile * 128 : tile * 128 + 128].T
        o_ref[:, 2 * cols + j, :] = jnp.concatenate([first[256:], second[256:]], axis=0).T


def layout(x):
    rows, cols, arcs = x.shape
    packed = 2 * cols + cols // 2
    return pl.pallas_call(
        layout_kernel,
        out_shape=jax.ShapeDtypeStruct((arcs, packed, 128), F32),
        compiler_params=pltpu.CompilerParams(vmem_limit_bytes=VMEM_LIMIT),
    )(x)


def local_kernel(counts_ref, l_ref, prior_ref, z_ref, info_ref, a_ref, q_ref, sign_ref):
    arcs, rows, loc = l_ref.shape
    place = lax.broadcasted_iota(jnp.int32, (rows, loc), 0)
    for b in range(arcs):
        masked = jnp.where(place < counts_ref[b], l_ref[b], 0.0)
        q_ref[b] = masked
        a_ref[b] = dot(masked, masked, TN, HI)
    cholesky_batch(a_ref)
    r = lax.broadcasted_iota(jnp.int32, (loc, loc), 0)
    l = lax.broadcasted_iota(jnp.int32, (loc, loc), 1)
    for b in range(arcs):
        basis = dot(q_ref[b], jnp.where(l <= r, a_ref[b], 0.0), NT, HI)
        q_ref[b] = basis
        a_ref[b] = basis[:loc]
    sign_ref[...] = jnp.zeros_like(sign_ref)

    def invert(p, carry):
        inverse_panel(a_ref, sign_ref, p)
        return carry

    lax.fori_loop(0, loc // 8, invert, 0)
    rest = rows - loc
    unit = (place == lax.broadcasted_iota(jnp.int32, (rows, loc), 1)).astype(F32)
    r2 = lax.broadcasted_iota(jnp.int32, (rest, rows), 0)
    l2 = lax.broadcasted_iota(jnp.int32, (rest, rows), 1)
    for b in range(arcs):
        q = q_ref[b]
        n = dot(q[loc:], a_ref[b], NN, HI)
        v = q * sign_ref[b][0:1] - unit
        keep = (l2 == r2 + loc) & (l2 < counts_ref[b])
        z = dot(n, v, NT, HI) + keep.astype(F32)
        zh, zl = split2(jnp.concatenate([z, z[:, 256:]], axis=1))
        z_ref[b, 0] = zh
        z_ref[b, 1] = zl
    half = prior_ref.shape[1] // 2
    for s in range(prior_ref.shape[0]):
        top = prior_ref[s, :half, :]
        low = prior_ref[s, :, half:]
        info_ref[s, :half, :] = dot(top[:, :half], top, TN, HI)
        info_ref[s, half:, half:] = dot(low, low, TN, HI)
        info_ref[s, half:, :half] = jnp.zeros((half, half), F32)


def local_part(counts, local_obs, prior):
    arcs, rows, loc = local_obs.shape
    vmem = pl.BlockSpec(memory_space=pltpu.VMEM)
    return pl.pallas_call(
        local_kernel,
        out_shape=(
            jax.ShapeDtypeStruct((arcs, 2, rows - loc, 384), BF16),
            jax.ShapeDtypeStruct(prior.shape, F32),
        ),
        in_specs=[pl.BlockSpec(memory_space=pltpu.SMEM), vmem, vmem],
        out_specs=(vmem, vmem),
        scratch_shapes=[
            pltpu.VMEM((arcs, loc, loc), F32),
            pltpu.VMEM((arcs, rows, loc), F32),
            pltpu.VMEM((arcs, 8, loc), F32),
        ],
        compiler_params=pltpu.CompilerParams(vmem_limit_bytes=VMEM_LIMIT),
    )(counts, local_obs, prior)


def eliminate_kernel(dest_ref, slot_ref, label_ref, g_ref, z_ref, o_ref, main_ref, tail_ref, sems, tail_sem):
    sources, _, packed, _ = g_ref.shape
    part = packed * 2 // 5
    half = part // 2
    width = sources * part
    a = pl.program_id(0)

    @pl.when(a == 0)
    def _():
        tail_ref[...] = jnp.zeros_like(tail_ref)
        tail_ref[:, width:, :] = jnp.full((tail_ref.shape[0], 8, 128), -1.0, F32)

    slot = slot_ref[a]
    dest = dest_ref[a]
    z = [jnp.concatenate([z_ref[0, i], jnp.zeros((64, 384), BF16)], axis=0) for i in range(2)]
    g = [g_ref[:, 0, i * part : (i + 1) * part, :].reshape(width, 128) for i in range(2)]
    t = g_ref[:, 0, 2 * part :, :].reshape(width // 2, 128)
    first = lax.broadcasted_iota(jnp.int32, t.shape, 1) < 64
    body = dot3(split2(jnp.concatenate(g, axis=1)), [w[:, :256] for w in z], NT)
    ends = [dot3(split2(jnp.where(own, t, 0.0)), [w[:, 256:] for w in z], NT) for own in (first, ~first)]
    ends = jnp.stack([e.reshape(sources, half, 256) for e in ends], axis=1).reshape(width, 256)
    r = body + ends
    main_ref[a] = r[:, :128]
    pltpu.make_async_copy(
        main_ref.at[a], o_ref.at[dest, pl.ds(pl.multiple_of(width * slot, 8), width), :], sems.at[a]
    ).start()
    tail_ref[dest, :width, :] += pltpu.roll(r[:, 128:], 64 * slot, 1)
    labels = tail_ref[dest, width:, :]
    at = lax.broadcasted_iota(jnp.int32, labels.shape, 0)
    tail_ref[dest, width:, :] = jnp.where(at == slot, label_ref[a].astype(F32), labels)

    @pl.when(a == pl.num_programs(0) - 1)
    def _():
        ends_copy = pltpu.make_async_copy(tail_ref, o_ref.at[:, 2 * width :, :], tail_sem)
        ends_copy.start()
        for b in range(main_ref.shape[0]):
            pltpu.make_async_copy(main_ref.at[b], o_ref.at[0, :width, :], sems.at[b]).wait()
        ends_copy.wait()


def eliminate(dest, slot, label, g, z, groups):
    sources, arcs, packed, _ = g.shape
    width = sources * packed * 2 // 5
    smem = pl.BlockSpec(memory_space=pltpu.SMEM)
    return pl.pallas_call(
        eliminate_kernel,
        out_shape=jax.ShapeDtypeStruct((groups, 3 * width + 8, 128), F32),
        grid=(arcs,),
        in_specs=[
            smem,
            smem,
            smem,
            pl.BlockSpec((sources, 1, packed, 128), lambda a: (0, a, 0, 0)),
            pl.BlockSpec((1, *z.shape[1:]), lambda a: (a, 0, 0, 0)),
        ],
        out_specs=pl.BlockSpec(memory_space=pl.ANY),
        scratch_shapes=[
            pltpu.VMEM((arcs, width, 128), F32),
            pltpu.VMEM((groups, width + 8, 128), F32),
            pltpu.SemaphoreType.DMA((arcs,)),
            pltpu.SemaphoreType.DMA,
        ],
        compiler_params=pltpu.CompilerParams(vmem_limit_bytes=VMEM_LIMIT),
    )(dest, slot, label, g, z)


def factor_kernel(x_ref, prior_ref, out_ref, info_ref, a_ref):
    slices, width, _ = prior_ref.shape
    half = width // 2
    n = pl.program_id(0)

    @pl.when(n == 0)
    def _():
        info_ref[...] = prior_ref[...]

    labels = x_ref[0, 3 * width :, :]
    for slot in range(2):
        label = labels[slot, 0].astype(jnp.int32)

        @pl.when(label >= 0)
        def _():
            tail = x_ref[0, 2 * width : 3 * width, :]
            own = lax.broadcasted_iota(jnp.int32, tail.shape, 1) // 64 == slot
            main = x_ref[0, slot * width : (slot + 1) * width, :]
            h, l = split2(jnp.concatenate([main, jnp.where(own, tail, 0.0)], axis=1))
            info_ref[label, :half, :] += dot3((h[:half], l[:half]), (h, l), NT)
            info_ref[label, half:, half:] += dot3((h[half:], l[half:]), (h[half:], l[half:]), NT)

    @pl.when(n == pl.num_programs(0) - 1)
    def _():
        r = lax.broadcasted_iota(jnp.int32, (128, 128), 0)
        l = lax.broadcasted_iota(jnp.int32, (128, 128), 1)
        for k in range(width // 128):
            lo, hi = 128 * k, 128 * k + 128
            a_ref[...] = info_ref[:, lo:hi, lo:hi]
            if k:
                out_ref[:, lo:hi, :lo] = jnp.zeros((slices, 128, lo), F32)

            def store(p, rows):
                out_ref[:, lo + 8 * p : lo + 8 * p + 8, lo:hi] = rows

            cholesky_blocks(a_ref, store)
            for s in range(slices if hi < width else 0):
                inverse = split2(jnp.where(l <= r, a_ref[s], 0.0))
                u = dot3(inverse, split2(info_ref[s, lo:hi, hi:]), NN)
                out_ref[s, lo:hi, hi:] = u
                uh, ul = split2(u)
                for j in range(0, width - hi, 128):
                    left = (uh[:, j : j + 128], ul[:, j : j + 128])
                    info_ref[s, hi + j : hi + j + 128, hi + j :] -= dot3(left, (uh[:, j:], ul[:, j:]), TN)


def factor(arrived, prior_gram):
    slices, width, _ = prior_gram.shape
    whole = pl.BlockSpec(prior_gram.shape, lambda n: (0, 0, 0))
    return pl.pallas_call(
        factor_kernel,
        out_shape=jax.ShapeDtypeStruct(prior_gram.shape, F32),
        grid=(arrived.shape[0],),
        in_specs=[pl.BlockSpec((1, *arrived.shape[1:]), lambda n: (n, 0, 0)), whole],
        out_specs=whole,
        scratch_shapes=[
            pltpu.VMEM((slices, width, width), F32),
            pltpu.VMEM((slices, 128, 128), F32),
        ],
        compiler_params=pltpu.CompilerParams(vmem_limit_bytes=VMEM_LIMIT),
    )(arrived, prior_gram)


def per_device(local_obs, global_obs, row_counts, owner_map, prior_factor):
    arc_dev = local_obs.shape[0]
    arc_groups = lax.axis_size("arc")
    col_groups = lax.axis_size("col")
    counts = lax.dynamic_slice_in_dim(row_counts, lax.axis_index("col") * arc_dev, arc_dev)
    packed = layout(jnp.transpose(global_obs, (1, 2, 0)))
    columns = lax.all_to_all(packed, "col", split_axis=0, concat_axis=0, tiled=True)
    columns = columns.reshape(col_groups, arc_dev, *packed.shape[1:])
    order = jnp.arange(arc_dev, dtype=jnp.int32)
    dest = owner_map // SLICE_DEV // col_groups
    earlier = (dest[None, :] == dest[:, None]) & (order[None, :] < order[:, None])
    slot = jnp.sum(earlier.astype(jnp.int32), axis=1)
    z, prior_gram = local_part(counts, local_obs, prior_factor)
    kept = eliminate(dest, slot, owner_map % SLICE_DEV, columns, z, arc_groups)
    arrived = lax.all_to_all(kept, "arc", split_axis=0, concat_axis=0, tiled=True)
    return factor(arrived, prior_gram)


def solution(mesh):
    placed = (
        P(("arc", "col"), None, None),
        P("arc", None, "col"),
        P("arc"),
        P(("arc", "col")),
        P(("arc", "col"), None, None),
    )
    return jax.shard_map(
        per_device,
        mesh=mesh,
        in_specs=placed,
        out_specs=P(("arc", "col"), None, None),
        check_vma=False,
    )
```

```python
import functools

import jax
import jax.numpy as jnp
from jax import lax
from jax.experimental import pallas as pl
from jax.experimental.pallas import tpu as pltpu
from jax.sharding import PartitionSpec as P

SLICE_DEV = 2
HI = lax.Precision.HIGHEST
F32 = jnp.float32
BF16 = jnp.bfloat16
NN = (((1,), (0,)), ((), ()))
NT = (((1,), (1,)), ((), ()))
TN = (((0,), (0,)), ((), ()))
VMEM_LIMIT = 60 * 1024 * 1024


def dot(a, b, dims, precision=None):
    return lax.dot_general(a, b, dims, precision=precision, preferred_element_type=F32)


def split2(x):
    high = x.astype(BF16)
    return high, (x - high.astype(F32)).astype(BF16)


def dot3(a, b, dims):
    ah, al = a
    bh, bl = b
    ka, kb = dims[0][0][0], dims[0][1][0]
    left = jnp.concatenate([ah, ah, al], axis=ka)
    return dot(left, jnp.concatenate([bh, bl, bh], axis=kb), dims)


def split3(x):
    high = x.astype(BF16).astype(F32)
    rest = x - high
    mid = rest.astype(BF16).astype(F32)
    return high, mid, rest - mid


def outer6(left, right):
    lh, lm, ll = split3(left)
    rh, rm, rl = split3(right)
    a = jnp.concatenate([lh, lh, lm, lh, ll, lm], axis=0).astype(BF16)
    b = jnp.concatenate([rh, rm, rh, rl, rh, rm], axis=0).astype(BF16)
    return dot(a, b, TN)


def outer3(left, right):
    lh, lm, _ = split3(left)
    rh, rm, _ = split3(right)
    a = jnp.concatenate([lh, lh, left - lh], axis=0).astype(BF16)
    b = jnp.concatenate([rh, right - rh, rh], axis=0).astype(BF16)
    return dot(a, b, TN)


def row_of(x, i):
    return jnp.broadcast_to(x[:, i : i + 1, :], x.shape)


def lane_of(x, i):
    return jnp.broadcast_to(x[:, :, i : i + 1], x.shape)


def panel_rows(p):
    return pl.ds(pl.multiple_of(8 * p, 8), 8)


def places(x, p):
    lane = lax.broadcasted_iota(jnp.int32, x.shape, 2) - 8 * p
    return lane, lax.broadcasted_iota(jnp.int32, x.shape, 1)


def columns_of(x, p):
    turned = pltpu.roll(x, lax.rem(128 - 8 * p, 128), 2)
    return [lane_of(turned, l) for l in range(8)]


def batch_panel(x, following, p):
    lane, sub = places(x, p)
    inside = (lane >= 0) & (lane < 8)
    c = columns_of(x, p)
    n = columns_of(following, p)
    place = jnp.where(inside, (lane == sub).astype(F32), x)
    following = jnp.where(inside, 0.0, following)
    pivots = x
    for i in range(8):
        d = row_of(c[i], i)
        inv = pl.reciprocal(d, approx=True)
        pivots = jnp.where(sub == i, d, pivots)
        below = jnp.where(sub > i, c[i], 0.0)
        below_n = n[i]
        for l in range(i + 1, 8):
            r = row_of(c[l], i)
            c[l] = c[l] - (below * r) * inv
            n[l] = n[l] - (below_n * r) * inv
        below = below * inv
        r = row_of(place, i)
        place = place - below * r
        following = following - (below_n * inv) * r
    scale = lax.rsqrt(pivots)
    return place * scale, following


def cholesky_batch(a_ref):
    count = a_ref.shape[0]

    def step(p, carry):
        left, right, x = carry
        a = a_ref[...]
        at_lane, at_row = places(a, p)
        t = jnp.stack([outer6(left[b], right[b]) for b in range(count)], axis=0)
        cleared = (at_lane < 0) & (at_lane >= -8) & (at_row >= 8 * p + 8)
        a_ref[...] = jnp.where(cleared, 0.0, a) - t
        following = a_ref[:, panel_rows(jnp.minimum(p + 1, 15)), :]
        place, following = batch_panel(x, following, p)
        lane, sub = places(x, p)
        a_ref[:, panel_rows(p), :] = place
        return jnp.where(lane >= 16, place, 0.0), place, following

    first = a_ref[:, :8, :]
    lax.fori_loop(0, 16, step, (jnp.zeros_like(first), jnp.zeros_like(first), first))


def columns_at(x, p):
    return [lane_of(x, 8 * p + l) for l in range(8)]


def cholesky_panel(x, c, following, p):
    lane, sub = places(x, p)
    inside = (lane >= 0) & (lane < 8)
    c = list(c)
    place = jnp.where(inside, (lane == sub).astype(F32), x)
    n = ahead = None
    if following is not None:
        n = columns_at(following, p)
        ahead = columns_at(following, p + 1)
        following = jnp.where(inside, 0.0, following)
    upper = x
    pivots = x
    for i in range(8):
        d = row_of(c[i], i)
        inv = pl.reciprocal(d, approx=True)
        pivots = jnp.where(sub == i, d, pivots)
        below = jnp.where(sub > i, c[i], 0.0)
        for l in range(i + 1, 8):
            r = row_of(c[l], i) * inv
            c[l] = c[l] - below * r
            if n is not None:
                n[l] = n[l] - n[i] * r
        r = row_of(place, i) * inv
        place = place - below * r
        if n is not None:
            following = following - n[i] * r
            less = n[i] * inv
            ahead = [ahead[l] - less * row_of(n[i], l) for l in range(8)]
        upper = upper - below * (row_of(upper, i) * inv)
    scale = lax.rsqrt(pivots)
    return upper * scale, place * scale, following, ahead


def cholesky_blocks(a_ref, store_upper):
    count = a_ref.shape[0]
    rows = [a_ref[:, 8 * q : 8 * q + 8, :] for q in range(16)]
    c = columns_at(rows[0], 0)
    for p in range(16):
        following = rows[p + 1] if p < 15 else None
        upper, place, following, c = cholesky_panel(rows[p], c, following, p)
        lane, sub = places(place, p)
        inside = (lane >= 0) & (lane < 8)
        a_ref[:, 8 * p : 8 * p + 8, :] = place
        if store_upper is not None:
            store_upper(p, jnp.where(lane >= sub, upper, 0.0))
        if p < 15:
            rows[p + 1] = following
        if p < 14:
            left = jnp.where(lane >= 16, place, 0.0)
            t = [outer3(left[b], place[b]) for b in range(count)]
            for q in range(p + 2, 16):
                part = jnp.stack([v[8 * q : 8 * q + 8] for v in t], axis=0)
                rows[q] = jnp.where(inside, 0.0, rows[q]) - part


def inverse_panel(a_ref, sign_ref, p):
    x = a_ref[:, panel_rows(p), :]
    lane, sub = places(x, p)
    c = columns_of(x, p)
    place = jnp.where((lane >= 0) & (lane < 8), (lane == sub).astype(F32), x)
    signs = sign_ref[...]
    for i in range(8):
        pv = row_of(c[i], i)
        s = jnp.where(pv >= 0.0, -1.0, 1.0)
        signs = jnp.where(lane == i, s, signs)
        inv = pl.reciprocal(pv - s, approx=True)
        lm = jnp.where(sub == i, 1.0 - inv, c[i] * inv)
        for l in range(i + 1, 8):
            c[l] = c[l] - lm * row_of(c[l], i)
        place = place - lm * row_of(place, i)
    sign_ref[...] = signs
    a = a_ref[...]
    at_lane, at_row = places(a, p)
    wide = jnp.concatenate([place] * 16, axis=1)
    factor = jnp.where((at_row >= 8 * p) & (at_row < 8 * p + 8), wide, 0.0)
    t = jnp.stack([dot(a[b], factor[b], NN, HI) for b in range(x.shape[0])], axis=0)
    a_ref[...] = jnp.where((at_lane >= 0) & (at_lane < 8), 0.0, a) - t
    a_ref[:, panel_rows(p), :] = place


def layout_kernel(x_ref, o_ref, x_buf, o_buf, in_sems, out_sems):
    rows, cols, arcs = x_ref.shape
    blocks = cols // 8
    arriving = []
    for b in range(blocks):
        copy = pltpu.make_async_copy(x_ref.at[:, 8 * b : 8 * b + 8, :], x_buf.at[b], in_sems.at[b])
        copy.start()
        arriving.append(copy)
    leaving = []

    def put(row, tiles):
        o_buf[:, row : row + 8, :] = jnp.transpose(tiles, (1, 0, 2))
        where = slice(row, row + 8)
        copy = pltpu.make_async_copy(o_buf.at[:, where, :], o_ref.at[:, where, :], out_sems.at[len(leaving)])
        copy.start()
        leaving.append(copy)

    ends = []
    for b in range(blocks):
        arriving[b].wait()
        for tile in range(2):
            v = jnp.transpose(x_buf[b, 128 * tile : 128 * tile + 128], (1, 0, 2))
            put(tile * cols + 8 * b, jnp.stack([v[c].T for c in range(8)], axis=0))
        ends.append(jnp.transpose(x_buf[b, 256:], (1, 0, 2)))
        if b % 2:
            both = jnp.concatenate(ends, axis=1)
            put(2 * cols + 4 * (b - 1), jnp.stack([both[c].T for c in range(8)], axis=0))
            ends = []
    for copy in leaving:
        copy.wait()


def layout(x):
    rows, cols, arcs = x.shape
    packed = 2 * cols + cols // 2
    hbm = pl.BlockSpec(memory_space=pltpu.HBM)
    return pl.pallas_call(
        layout_kernel,
        out_shape=jax.ShapeDtypeStruct((arcs, packed, 128), F32),
        in_specs=[hbm],
        out_specs=hbm,
        scratch_shapes=[
            pltpu.VMEM((cols // 8, rows, 8, arcs), F32),
            pltpu.VMEM((arcs, packed, 128), F32),
            pltpu.SemaphoreType.DMA((cols // 8,)),
            pltpu.SemaphoreType.DMA((packed // 8,)),
        ],
        compiler_params=pltpu.CompilerParams(vmem_limit_bytes=VMEM_LIMIT),
    )(x)


def local_kernel(counts_ref, l_ref, prior_ref, z_ref, info_ref, a_ref, q_ref, sign_ref):
    arcs, rows, loc = l_ref.shape
    place = lax.broadcasted_iota(jnp.int32, (rows, loc), 0)
    for b in range(arcs):
        masked = jnp.where(place < counts_ref[b], l_ref[b], 0.0)
        q_ref[b] = masked
        a_ref[b] = dot(masked, masked, TN, HI)
    cholesky_batch(a_ref)
    r = lax.broadcasted_iota(jnp.int32, (loc, loc), 0)
    l = lax.broadcasted_iota(jnp.int32, (loc, loc), 1)
    for b in range(arcs):
        basis = dot(q_ref[b], jnp.where(l <= r, a_ref[b], 0.0), NT, HI)
        q_ref[b] = basis
        a_ref[b] = basis[:loc]
    sign_ref[...] = jnp.zeros_like(sign_ref)

    def invert(p, carry):
        inverse_panel(a_ref, sign_ref, p)
        return carry

    lax.fori_loop(0, loc // 8, invert, 0)
    rest = rows - loc
    unit = (place == lax.broadcasted_iota(jnp.int32, (rows, loc), 1)).astype(F32)
    r2 = lax.broadcasted_iota(jnp.int32, (rest, rows), 0)
    l2 = lax.broadcasted_iota(jnp.int32, (rest, rows), 1)
    for b in range(arcs):
        q = q_ref[b]
        n = dot(q[loc:], a_ref[b], NN, HI)
        v = q * sign_ref[b][0:1] - unit
        keep = (l2 == r2 + loc) & (l2 < counts_ref[b])
        z = dot(n, v, NT, HI) + keep.astype(F32)
        zh, zl = split2(jnp.concatenate([z, z[:, 256:]], axis=1))
        z_ref[b, 0] = zh
        z_ref[b, 1] = zl
    half = prior_ref.shape[1] // 2
    for s in range(prior_ref.shape[0]):
        top = prior_ref[s, :half, :]
        low = prior_ref[s, :, half:]
        info_ref[s, :half, :] = dot(top[:, :half], top, TN, HI)
        info_ref[s, half:, half:] = dot(low, low, TN, HI)
        info_ref[s, half:, :half] = jnp.zeros((half, half), F32)


def local_part(counts, local_obs, prior):
    arcs, rows, loc = local_obs.shape
    vmem = pl.BlockSpec(memory_space=pltpu.VMEM)
    return pl.pallas_call(
        local_kernel,
        out_shape=(
            jax.ShapeDtypeStruct((arcs, 2, rows - loc, 384), BF16),
            jax.ShapeDtypeStruct(prior.shape, F32),
        ),
        in_specs=[pl.BlockSpec(memory_space=pltpu.SMEM), vmem, vmem],
        out_specs=(vmem, vmem),
        scratch_shapes=[
            pltpu.VMEM((arcs, loc, loc), F32),
            pltpu.VMEM((arcs, rows, loc), F32),
            pltpu.VMEM((arcs, 8, loc), F32),
        ],
        compiler_params=pltpu.CompilerParams(vmem_limit_bytes=VMEM_LIMIT),
    )(counts, local_obs, prior)


def eliminate_kernel(
    dest_ref, slot_ref, label_ref, g_hbm, z_hbm, o_ref, g_buf, z_buf, main_ref, tail_ref, g_sems, z_sems, sems, tail_sem
):
    arcs, sources, packed, _ = g_buf.shape
    part = packed * 2 // 5
    width = sources * part

    def columns(a):
        return pltpu.make_async_copy(g_hbm.at[:, a], g_buf.at[a], g_sems.at[a])

    def weights(a):
        return pltpu.make_async_copy(z_hbm.at[a], z_buf.at[a], z_sems.at[a])

    for a in range(arcs):
        columns(a).start()
        weights(a).start()
    tail_ref[...] = jnp.zeros_like(tail_ref)
    tail_ref[:, width:, :] = jnp.full((tail_ref.shape[0], 8, 128), -1.0, F32)

    def arc(a, carry):
        slot = slot_ref[a]
        dest = dest_ref[a]
        columns(a).wait()
        weights(a).wait()
        g = [g_buf[a, :, i * part : (i + 1) * part, :].reshape(width, 128) for i in range(2)]
        t = g_buf[a, :, 2 * part :, :].reshape(width // 16, 8, 128)
        first = lax.broadcasted_iota(jnp.int32, t.shape, 2) < 64
        ends = jnp.stack([jnp.where(own, t, 0.0) for own in (first, ~first)], axis=1).reshape(width, 128)
        zh, zl = [jnp.concatenate([z_buf[a, i], jnp.zeros((64, 384), BF16)], axis=0) for i in range(2)]
        r = dot3(split2(jnp.concatenate([*g, ends], axis=1)), (zh, zl), NT)
        main_ref[a] = r[:, :128]
        pltpu.make_async_copy(
            main_ref.at[a], o_ref.at[dest, pl.ds(pl.multiple_of(width * slot, 8), width), :], sems.at[a]
        ).start()
        tail_ref[dest, :width, :] += pltpu.roll(r[:, 128:], 64 * slot, 1)
        labels = tail_ref[dest, width:, :]
        at = lax.broadcasted_iota(jnp.int32, labels.shape, 0)
        tail_ref[dest, width:, :] = jnp.where(at == slot, label_ref[a].astype(F32), labels)
        return carry

    lax.fori_loop(0, arcs, arc, 0)
    ends_copy = pltpu.make_async_copy(tail_ref, o_ref.at[:, 2 * width :, :], tail_sem)
    ends_copy.start()
    for a in range(arcs):
        pltpu.make_async_copy(main_ref.at[a], o_ref.at[0, :width, :], sems.at[a]).wait()
    ends_copy.wait()


def eliminate(dest, slot, label, g, z, groups):
    sources, arcs, packed, _ = g.shape
    width = sources * packed * 2 // 5
    smem = pl.BlockSpec(memory_space=pltpu.SMEM)
    hbm = pl.BlockSpec(memory_space=pltpu.HBM)
    return pl.pallas_call(
        eliminate_kernel,
        out_shape=jax.ShapeDtypeStruct((groups, 3 * width + 8, 128), F32),
        in_specs=[smem, smem, smem, hbm, hbm],
        out_specs=hbm,
        scratch_shapes=[
            pltpu.VMEM((arcs, sources, packed, 128), F32),
            pltpu.VMEM(z.shape, BF16),
            pltpu.VMEM((arcs, width, 128), F32),
            pltpu.VMEM((groups, width + 8, 128), F32),
            pltpu.SemaphoreType.DMA((arcs,)),
            pltpu.SemaphoreType.DMA((arcs,)),
            pltpu.SemaphoreType.DMA((arcs,)),
            pltpu.SemaphoreType.DMA,
        ],
        compiler_params=pltpu.CompilerParams(vmem_limit_bytes=VMEM_LIMIT),
    )(dest, slot, label, g, z)


def factor_kernel(x_hbm, prior_ref, out_hbm, x_buf, info_ref, out_ref, a_ref, sems, prior_sem, out_sems):
    slices, width, _ = info_ref.shape
    groups = x_buf.shape[0]
    half = width // 2

    def rows_of(n):
        return pltpu.make_async_copy(x_hbm.at[n], x_buf.at[n], sems.at[n])

    start = pltpu.make_async_copy(prior_ref, info_ref, prior_sem)
    start.start()
    for n in range(groups):
        rows_of(n).start()
    start.wait()

    def add(n, carry):
        rows_of(n).wait()
        labels = x_buf[n, 3 * width :, :]
        for slot in range(2):
            label = labels[slot, 0].astype(jnp.int32)

            @pl.when(label >= 0)
            def _():
                tail = x_buf[n, 2 * width : 3 * width, :]
                own = lax.broadcasted_iota(jnp.int32, tail.shape, 1) // 64 == slot
                main = x_buf[n, slot * width : (slot + 1) * width, :]
                h, l = split2(jnp.concatenate([main, jnp.where(own, tail, 0.0)], axis=1))
                info_ref[label, :half, :] += dot3((h[:half], l[:half]), (h, l), NT)
                info_ref[label, half:, half:] += dot3((h[half:], l[half:]), (h[half:], l[half:]), NT)

        return carry

    lax.fori_loop(0, groups, add, 0)
    r = lax.broadcasted_iota(jnp.int32, (128, 128), 0)
    l = lax.broadcasted_iota(jnp.int32, (128, 128), 1)
    leaving = []
    for k in range(width // 128):
        lo, hi = 128 * k, 128 * k + 128
        a_ref[...] = info_ref[:, lo:hi, lo:hi]
        if k:
            out_ref[:, lo:hi, :lo] = jnp.zeros((slices, 128, lo), F32)

        def store(p, rows):
            out_ref[:, lo + 8 * p : lo + 8 * p + 8, lo:hi] = rows

        cholesky_blocks(a_ref, store)
        for s in range(slices if hi < width else 0):
            inverse = split2(jnp.where(l <= r, a_ref[s], 0.0))
            u = dot3(inverse, split2(info_ref[s, lo:hi, hi:]), NN)
            out_ref[s, lo:hi, hi:] = u
            uh, ul = split2(u)
            for j in range(0, width - hi, 128):
                left = (uh[:, j : j + 128], ul[:, j : j + 128])
                info_ref[s, hi + j : hi + j + 128, hi + j :] -= dot3(left, (uh[:, j:], ul[:, j:]), TN)
        copy = pltpu.make_async_copy(out_ref.at[:, lo:hi, :], out_hbm.at[:, lo:hi, :], out_sems.at[k])
        copy.start()
        leaving.append(copy)
    for copy in leaving:
        copy.wait()


def factor(arrived, prior_gram):
    slices, width, _ = prior_gram.shape
    hbm = pl.BlockSpec(memory_space=pltpu.HBM)
    return pl.pallas_call(
        factor_kernel,
        out_shape=jax.ShapeDtypeStruct(prior_gram.shape, F32),
        in_specs=[hbm, pl.BlockSpec(memory_space=pl.ANY)],
        out_specs=hbm,
        scratch_shapes=[
            pltpu.VMEM(arrived.shape, F32),
            pltpu.VMEM((slices, width, width), F32),
            pltpu.VMEM((slices, width, width), F32),
            pltpu.VMEM((slices, 128, 128), F32),
            pltpu.SemaphoreType.DMA((arrived.shape[0],)),
            pltpu.SemaphoreType.DMA,
            pltpu.SemaphoreType.DMA((width // 128,)),
        ],
        compiler_params=pltpu.CompilerParams(vmem_limit_bytes=VMEM_LIMIT),
    )(arrived, prior_gram)


def per_device(local_obs, global_obs, row_counts, owner_map, prior_factor):
    arc_dev = local_obs.shape[0]
    arc_groups = lax.axis_size("arc")
    col_groups = lax.axis_size("col")
    counts = lax.dynamic_slice_in_dim(row_counts, lax.axis_index("col") * arc_dev, arc_dev)
    packed = layout(jnp.transpose(global_obs, (1, 2, 0)))
    columns = lax.all_to_all(packed, "col", split_axis=0, concat_axis=0, tiled=True)
    columns = columns.reshape(col_groups, arc_dev, *packed.shape[1:])
    order = jnp.arange(arc_dev, dtype=jnp.int32)
    dest = owner_map // SLICE_DEV // col_groups
    earlier = (dest[None, :] == dest[:, None]) & (order[None, :] < order[:, None])
    slot = jnp.sum(earlier.astype(jnp.int32), axis=1)
    z, prior_gram = local_part(counts, local_obs, prior_factor)
    kept = eliminate(dest, slot, owner_map % SLICE_DEV, columns, z, arc_groups)
    arrived = lax.all_to_all(kept, "arc", split_axis=0, concat_axis=0, tiled=True)
    return factor(arrived, prior_gram)


def solution(mesh):
    placed = (
        P(("arc", "col"), None, None),
        P("arc", None, "col"),
        P("arc"),
        P(("arc", "col")),
        P(("arc", "col"), None, None),
    )
    return jax.shard_map(
        per_device,
        mesh=mesh,
        in_specs=placed,
        out_specs=P(("arc", "col"), None, None),
        check_vma=False,
    )
```

```python
import functools

import jax
import jax.numpy as jnp
from jax import lax
from jax.experimental import pallas as pl
from jax.experimental.pallas import tpu as pltpu
from jax.sharding import PartitionSpec as P

SLICE_DEV = 2
HI = lax.Precision.HIGHEST
F32 = jnp.float32
BF16 = jnp.bfloat16
NN = (((1,), (0,)), ((), ()))
NT = (((1,), (1,)), ((), ()))
TN = (((0,), (0,)), ((), ()))
CHUNKS = 2
VMEM_LIMIT = 60 * 1024 * 1024


def dot(a, b, dims, precision=None):
    return lax.dot_general(a, b, dims, precision=precision, preferred_element_type=F32)


def split2(x):
    high = x.astype(BF16)
    return high, (x - high.astype(F32)).astype(BF16)


def dot3(a, b, dims):
    ah, al = a
    bh, bl = b
    ka, kb = dims[0][0][0], dims[0][1][0]
    left = jnp.concatenate([ah, ah, al], axis=ka)
    return dot(left, jnp.concatenate([bh, bl, bh], axis=kb), dims)


def split3(x):
    high = x.astype(BF16).astype(F32)
    rest = x - high
    mid = rest.astype(BF16).astype(F32)
    return high, mid, rest - mid


def outer6(left, right):
    lh, lm, ll = split3(left)
    rh, rm, rl = split3(right)
    a = jnp.concatenate([lh, lh, lm, lh, ll, lm], axis=0).astype(BF16)
    b = jnp.concatenate([rh, rm, rh, rl, rh, rm], axis=0).astype(BF16)
    return dot(a, b, TN)


def outer3(left, right):
    lh, lm, _ = split3(left)
    rh, rm, _ = split3(right)
    a = jnp.concatenate([lh, lh, left - lh], axis=0).astype(BF16)
    b = jnp.concatenate([rh, right - rh, rh], axis=0).astype(BF16)
    return dot(a, b, TN)


def row_of(x, i):
    return jnp.broadcast_to(x[:, i : i + 1, :], x.shape)


def lane_of(x, i):
    return jnp.broadcast_to(x[:, :, i : i + 1], x.shape)


def panel_rows(p):
    return pl.ds(pl.multiple_of(8 * p, 8), 8)


def places(x, p):
    lane = lax.broadcasted_iota(jnp.int32, x.shape, 2) - 8 * p
    return lane, lax.broadcasted_iota(jnp.int32, x.shape, 1)


def columns_of(x, p):
    turned = pltpu.roll(x, lax.rem(128 - 8 * p, 128), 2)
    return [lane_of(turned, l) for l in range(8)]


def batch_panel(x, following, p):
    lane, sub = places(x, p)
    inside = (lane >= 0) & (lane < 8)
    c = columns_of(x, p)
    n = columns_of(following, p)
    place = jnp.where(inside, (lane == sub).astype(F32), x)
    following = jnp.where(inside, 0.0, following)
    pivots = x
    for i in range(8):
        d = row_of(c[i], i)
        inv = pl.reciprocal(d, approx=True)
        pivots = jnp.where(sub == i, d, pivots)
        below = jnp.where(sub > i, c[i], 0.0)
        below_n = n[i]
        for l in range(i + 1, 8):
            r = row_of(c[l], i)
            c[l] = c[l] - (below * r) * inv
            n[l] = n[l] - (below_n * r) * inv
        below = below * inv
        r = row_of(place, i)
        place = place - below * r
        following = following - (below_n * inv) * r
    scale = lax.rsqrt(pivots)
    return place * scale, following


def cholesky_batch(a_ref):
    count = a_ref.shape[0]

    def step(p, carry):
        left, right, x = carry
        a = a_ref[...]
        at_lane, at_row = places(a, p)
        t = jnp.stack([outer6(left[b], right[b]) for b in range(count)], axis=0)
        cleared = (at_lane < 0) & (at_lane >= -8) & (at_row >= 8 * p + 8)
        a_ref[...] = jnp.where(cleared, 0.0, a) - t
        following = a_ref[:, panel_rows(jnp.minimum(p + 1, 15)), :]
        place, following = batch_panel(x, following, p)
        lane, sub = places(x, p)
        a_ref[:, panel_rows(p), :] = place
        return jnp.where(lane >= 16, place, 0.0), place, following

    first = a_ref[:, :8, :]
    lax.fori_loop(0, 16, step, (jnp.zeros_like(first), jnp.zeros_like(first), first))


def columns_at(x, p):
    return [lane_of(x, 8 * p + l) for l in range(8)]


def cholesky_panel(x, c, following, p):
    lane, sub = places(x, p)
    inside = (lane >= 0) & (lane < 8)
    c = list(c)
    place = jnp.where(inside, (lane == sub).astype(F32), x)
    n = ahead = None
    if following is not None:
        n = columns_at(following, p)
        ahead = columns_at(following, p + 1)
        following = jnp.where(inside, 0.0, following)
    upper = x
    pivots = x
    for i in range(8):
        d = row_of(c[i], i)
        inv = pl.reciprocal(d, approx=True)
        pivots = jnp.where(sub == i, d, pivots)
        below = jnp.where(sub > i, c[i], 0.0)
        for l in range(i + 1, 8):
            r = row_of(c[l], i) * inv
            c[l] = c[l] - below * r
            if n is not None:
                n[l] = n[l] - n[i] * r
        r = row_of(place, i) * inv
        place = place - below * r
        if n is not None:
            following = following - n[i] * r
            less = n[i] * inv
            ahead = [ahead[l] - less * row_of(n[i], l) for l in range(8)]
        upper = upper - below * (row_of(upper, i) * inv)
    scale = lax.rsqrt(pivots)
    return upper * scale, place * scale, following, ahead


def cholesky_blocks(a_ref, store_upper):
    count = a_ref.shape[0]
    rows = [a_ref[:, 8 * q : 8 * q + 8, :] for q in range(16)]
    c = columns_at(rows[0], 0)
    for p in range(16):
        following = rows[p + 1] if p < 15 else None
        upper, place, following, c = cholesky_panel(rows[p], c, following, p)
        lane, sub = places(place, p)
        inside = (lane >= 0) & (lane < 8)
        a_ref[:, 8 * p : 8 * p + 8, :] = place
        if store_upper is not None:
            store_upper(p, jnp.where(lane >= sub, upper, 0.0))
        if p < 15:
            rows[p + 1] = following
        if p < 14:
            left = jnp.where(lane >= 16, place, 0.0)
            t = [outer3(left[b], place[b]) for b in range(count)]
            for q in range(p + 2, 16):
                part = jnp.stack([v[8 * q : 8 * q + 8] for v in t], axis=0)
                rows[q] = jnp.where(inside, 0.0, rows[q]) - part


def inverse_panel(a_ref, sign_ref, p):
    x = a_ref[:, panel_rows(p), :]
    lane, sub = places(x, p)
    c = columns_of(x, p)
    place = jnp.where((lane >= 0) & (lane < 8), (lane == sub).astype(F32), x)
    signs = sign_ref[...]
    for i in range(8):
        pv = row_of(c[i], i)
        s = jnp.where(pv >= 0.0, -1.0, 1.0)
        signs = jnp.where(lane == i, s, signs)
        inv = pl.reciprocal(pv - s, approx=True)
        lm = jnp.where(sub == i, 1.0 - inv, c[i] * inv)
        for l in range(i + 1, 8):
            c[l] = c[l] - lm * row_of(c[l], i)
        place = place - lm * row_of(place, i)
    sign_ref[...] = signs
    a = a_ref[...]
    at_lane, at_row = places(a, p)
    wide = jnp.concatenate([place] * 16, axis=1)
    factor = jnp.where((at_row >= 8 * p) & (at_row < 8 * p + 8), wide, 0.0)
    t = jnp.stack([dot(a[b], factor[b], NN, HI) for b in range(x.shape[0])], axis=0)
    a_ref[...] = jnp.where((at_lane >= 0) & (at_lane < 8), 0.0, a) - t
    a_ref[:, panel_rows(p), :] = place


def layout_kernel(chunk, x_ref, *refs):
    o_ref, x_buf, o_buf, in_sems, out_sems = refs[-5:]
    blocks, rows, _, arcs = x_buf.shape
    cols = 8 * blocks
    arriving = []
    for b in range(blocks):
        columns = slice(chunk * cols + 8 * b, chunk * cols + 8 * b + 8)
        copy = pltpu.make_async_copy(x_ref.at[:, columns, :], x_buf.at[b], in_sems.at[b])
        copy.start()
        arriving.append(copy)
    leaving = []

    def put(row, tiles):
        o_buf[:, row : row + 8, :] = jnp.transpose(tiles, (1, 0, 2))
        where = slice(row, row + 8)
        copy = pltpu.make_async_copy(o_buf.at[:, where, :], o_ref.at[:, where, :], out_sems.at[len(leaving)])
        copy.start()
        leaving.append(copy)

    ends = []
    for b in range(blocks):
        arriving[b].wait()
        for tile in range(2):
            v = jnp.transpose(x_buf[b, 128 * tile : 128 * tile + 128], (1, 0, 2))
            put(tile * cols + 8 * b, jnp.stack([v[c].T for c in range(8)], axis=0))
        ends.append(jnp.transpose(x_buf[b, 256:], (1, 0, 2)))
        if b % 2:
            both = jnp.concatenate(ends, axis=1)
            put(2 * cols + 4 * (b - 1), jnp.stack([both[c].T for c in range(8)], axis=0))
            ends = []
    for copy in leaving:
        copy.wait()


def layout(x, chunk, after=()):
    rows, cols, arcs = x.shape
    cols = cols // CHUNKS
    packed = 2 * cols + cols // 2
    hbm = pl.BlockSpec(memory_space=pltpu.HBM)
    return pl.pallas_call(
        functools.partial(layout_kernel, chunk),
        out_shape=jax.ShapeDtypeStruct((arcs, packed, 128), F32),
        in_specs=[hbm] + [pl.BlockSpec(memory_space=pl.ANY)] * len(after),
        out_specs=hbm,
        scratch_shapes=[
            pltpu.VMEM((cols // 8, rows, 8, arcs), F32),
            pltpu.VMEM((arcs, packed, 128), F32),
            pltpu.SemaphoreType.DMA((cols // 8,)),
            pltpu.SemaphoreType.DMA((packed // 8,)),
        ],
        compiler_params=pltpu.CompilerParams(vmem_limit_bytes=VMEM_LIMIT),
    )(x, *after)


def local_kernel(counts_ref, l_ref, prior_ref, z_ref, info_ref, a_ref, q_ref, sign_ref):
    arcs, rows, loc = l_ref.shape
    place = lax.broadcasted_iota(jnp.int32, (rows, loc), 0)
    for b in range(arcs):
        masked = jnp.where(place < counts_ref[b], l_ref[b], 0.0)
        q_ref[b] = masked
        a_ref[b] = dot(masked, masked, TN, HI)
    cholesky_batch(a_ref)
    r = lax.broadcasted_iota(jnp.int32, (loc, loc), 0)
    l = lax.broadcasted_iota(jnp.int32, (loc, loc), 1)
    for b in range(arcs):
        basis = dot(q_ref[b], jnp.where(l <= r, a_ref[b], 0.0), NT, HI)
        q_ref[b] = basis
        a_ref[b] = basis[:loc]
    sign_ref[...] = jnp.zeros_like(sign_ref)

    def invert(p, carry):
        inverse_panel(a_ref, sign_ref, p)
        return carry

    lax.fori_loop(0, loc // 8, invert, 0)
    rest = rows - loc
    unit = (place == lax.broadcasted_iota(jnp.int32, (rows, loc), 1)).astype(F32)
    r2 = lax.broadcasted_iota(jnp.int32, (rest, rows), 0)
    l2 = lax.broadcasted_iota(jnp.int32, (rest, rows), 1)
    for b in range(arcs):
        q = q_ref[b]
        n = dot(q[loc:], a_ref[b], NN, HI)
        v = q * sign_ref[b][0:1] - unit
        keep = (l2 == r2 + loc) & (l2 < counts_ref[b])
        z = dot(n, v, NT, HI) + keep.astype(F32)
        zh, zl = split2(jnp.concatenate([z, z[:, 256:]], axis=1))
        z_ref[b, 0] = zh
        z_ref[b, 1] = zl
    half = prior_ref.shape[1] // 2
    for s in range(prior_ref.shape[0]):
        top = prior_ref[s, :half, :]
        low = prior_ref[s, :, half:]
        info_ref[s, :half, :] = dot(top[:, :half], top, TN, HI)
        info_ref[s, half:, half:] = dot(low, low, TN, HI)
        info_ref[s, half:, :half] = jnp.zeros((half, half), F32)


def local_part(counts, local_obs, prior):
    arcs, rows, loc = local_obs.shape
    vmem = pl.BlockSpec(memory_space=pltpu.VMEM)
    return pl.pallas_call(
        local_kernel,
        out_shape=(
            jax.ShapeDtypeStruct((arcs, 2, rows - loc, 384), BF16),
            jax.ShapeDtypeStruct(prior.shape, F32),
        ),
        in_specs=[pl.BlockSpec(memory_space=pltpu.SMEM), vmem, vmem],
        out_specs=(vmem, vmem),
        scratch_shapes=[
            pltpu.VMEM((arcs, loc, loc), F32),
            pltpu.VMEM((arcs, rows, loc), F32),
            pltpu.VMEM((arcs, 8, loc), F32),
        ],
        compiler_params=pltpu.CompilerParams(vmem_limit_bytes=VMEM_LIMIT),
    )(counts, local_obs, prior)


def eliminate_kernel(dest_ref, slot_ref, label_ref, *refs):
    g_hbm = refs[:CHUNKS]
    z_hbm, o_ref, g_buf, z_buf, main_ref, tail_ref, g_sems, z_sems, sems, tail_sem = refs[CHUNKS:]
    arcs, sources, packed, _ = g_buf.shape
    part = packed * 2 // 5
    width = sources * part

    def columns(a):
        copies = []
        for h in range(CHUNKS):
            at = 0
            for piece, size in enumerate((part // CHUNKS, part // CHUNKS, part // 2 // CHUNKS)):
                copies.append(
                    pltpu.make_async_copy(
                        g_hbm[h].at[:, a, at : at + size, :],
                        g_buf.at[a, :, piece * part + h * size : piece * part + h * size + size, :],
                        g_sems.at[a, 3 * h + piece],
                    )
                )
                at += size
        return copies

    def weights(a):
        return pltpu.make_async_copy(z_hbm.at[a], z_buf.at[a], z_sems.at[a])

    for a in range(arcs):
        for copy in columns(a):
            copy.start()
        weights(a).start()
    tail_ref[...] = jnp.zeros_like(tail_ref)
    tail_ref[:, width:, :] = jnp.full((tail_ref.shape[0], 8, 128), -1.0, F32)

    def arc(a, carry):
        slot = slot_ref[a]
        dest = dest_ref[a]
        for copy in columns(a):
            copy.wait()
        weights(a).wait()
        g = [g_buf[a, :, i * part : (i + 1) * part, :].reshape(width, 128) for i in range(2)]
        t = g_buf[a, :, 2 * part :, :].reshape(width // 16, 8, 128)
        first = lax.broadcasted_iota(jnp.int32, t.shape, 2) < 64
        ends = jnp.stack([jnp.where(own, t, 0.0) for own in (first, ~first)], axis=1).reshape(width, 128)
        zh, zl = [jnp.concatenate([z_buf[a, i], jnp.zeros((64, 384), BF16)], axis=0) for i in range(2)]
        r = dot3(split2(jnp.concatenate([*g, ends], axis=1)), (zh, zl), NT)
        main_ref[a] = r[:, :128]
        pltpu.make_async_copy(
            main_ref.at[a], o_ref.at[dest, pl.ds(pl.multiple_of(width * slot, 8), width), :], sems.at[a]
        ).start()
        tail_ref[dest, :width, :] += pltpu.roll(r[:, 128:], 64 * slot, 1)
        labels = tail_ref[dest, width:, :]
        at = lax.broadcasted_iota(jnp.int32, labels.shape, 0)
        tail_ref[dest, width:, :] = jnp.where(at == slot, label_ref[a].astype(F32), labels)
        return carry

    lax.fori_loop(0, arcs, arc, 0)
    ends_copy = pltpu.make_async_copy(tail_ref, o_ref.at[:, 2 * width :, :], tail_sem)
    ends_copy.start()
    for a in range(arcs):
        pltpu.make_async_copy(main_ref.at[a], o_ref.at[0, :width, :], sems.at[a]).wait()
    ends_copy.wait()


def eliminate(dest, slot, label, g, z, groups):
    sources, arcs, packed, _ = g[0].shape
    packed = packed * CHUNKS
    width = sources * packed * 2 // 5
    smem = pl.BlockSpec(memory_space=pltpu.SMEM)
    hbm = pl.BlockSpec(memory_space=pltpu.HBM)
    return pl.pallas_call(
        eliminate_kernel,
        out_shape=jax.ShapeDtypeStruct((groups, 3 * width + 8, 128), F32),
        in_specs=[smem, smem, smem] + [hbm] * (CHUNKS + 1),
        out_specs=hbm,
        scratch_shapes=[
            pltpu.VMEM((arcs, sources, packed, 128), F32),
            pltpu.VMEM(z.shape, BF16),
            pltpu.VMEM((arcs, width, 128), F32),
            pltpu.VMEM((groups, width + 8, 128), F32),
            pltpu.SemaphoreType.DMA((arcs, 3 * CHUNKS)),
            pltpu.SemaphoreType.DMA((arcs,)),
            pltpu.SemaphoreType.DMA((arcs,)),
            pltpu.SemaphoreType.DMA,
        ],
        compiler_params=pltpu.CompilerParams(vmem_limit_bytes=VMEM_LIMIT),
    )(dest, slot, label, *g, z)


def factor_kernel(x_hbm, prior_ref, out_hbm, list_ref, x_buf, info_ref, out_ref, a_ref, sems, prior_sem, out_sems):
    slices, width, _ = info_ref.shape
    groups = x_buf.shape[0] - 1
    half = width // 2

    def rows_of(n):
        return pltpu.make_async_copy(x_hbm.at[n], x_buf.at[n], sems.at[n])

    start = pltpu.make_async_copy(prior_ref, info_ref, prior_sem)
    start.start()
    for n in range(groups):
        rows_of(n).start()
    x_buf[groups] = jnp.zeros_like(x_buf[groups])
    start.wait()

    def listed(n, count):
        rows_of(n).wait()
        labels = x_buf[n, 3 * width :, :]
        for slot in range(2):
            label = labels[slot, 0].astype(jnp.int32)
            list_ref[0, count] = n
            list_ref[1, count] = slot
            list_ref[2, count] = label
            count = count + (label >= 0).astype(jnp.int32)
        return count

    count = lax.fori_loop(0, groups, listed, 0)
    list_ref[0, count] = groups
    list_ref[1, count] = 0
    list_ref[2, count] = 0

    def add(pair, carry):
        items = []
        for i in range(2):
            n, slot = list_ref[0, 2 * pair + i], list_ref[1, 2 * pair + i]
            main = x_buf[n, pl.ds(pl.multiple_of(slot * width, 8), width), :]
            tail = x_buf[n, 2 * width : 3 * width, :]
            own = lax.broadcasted_iota(jnp.int32, tail.shape, 1) // 64 == slot
            h, l = split2(jnp.concatenate([main, jnp.where(own, tail, 0.0)], axis=1))
            top = dot3((h[:half], l[:half]), (h, l), NT)
            items.append((list_ref[2, 2 * pair + i], top, dot3((h[half:], l[half:]), (h[half:], l[half:]), NT)))
        for label, top, low in items:
            info_ref[label, :half, :] += top
            info_ref[label, half:, half:] += low
        return carry

    lax.fori_loop(0, (count + 1) // 2, add, 0)
    r = lax.broadcasted_iota(jnp.int32, (128, 128), 0)
    l = lax.broadcasted_iota(jnp.int32, (128, 128), 1)
    leaving = []
    for k in range(width // 128):
        lo, hi = 128 * k, 128 * k + 128
        a_ref[...] = info_ref[:, lo:hi, lo:hi]
        if k:
            out_ref[:, lo:hi, :lo] = jnp.zeros((slices, 128, lo), F32)

        def store(p, rows):
            out_ref[:, lo + 8 * p : lo + 8 * p + 8, lo:hi] = rows

        cholesky_blocks(a_ref, store)
        for s in range(slices if hi < width else 0):
            inverse = split2(jnp.where(l <= r, a_ref[s], 0.0))
            u = dot3(inverse, split2(info_ref[s, lo:hi, hi:]), NN)
            out_ref[s, lo:hi, hi:] = u
            uh, ul = split2(u)
            for j in range(0, width - hi, 128):
                left = (uh[:, j : j + 128], ul[:, j : j + 128])
                info_ref[s, hi + j : hi + j + 128, hi + j :] -= dot3(left, (uh[:, j:], ul[:, j:]), TN)
        copy = pltpu.make_async_copy(out_ref.at[:, lo:hi, :], out_hbm.at[:, lo:hi, :], out_sems.at[k])
        copy.start()
        leaving.append(copy)
    for copy in leaving:
        copy.wait()


def factor(arrived, prior_gram):
    slices, width, _ = prior_gram.shape
    hbm = pl.BlockSpec(memory_space=pltpu.HBM)
    return pl.pallas_call(
        factor_kernel,
        out_shape=jax.ShapeDtypeStruct(prior_gram.shape, F32),
        in_specs=[hbm, pl.BlockSpec(memory_space=pl.ANY)],
        out_specs=hbm,
        scratch_shapes=[
            pltpu.SMEM((3, 2 * arrived.shape[0] + 1), jnp.int32),
            pltpu.VMEM((arrived.shape[0] + 1, *arrived.shape[1:]), F32),
            pltpu.VMEM((slices, width, width), F32),
            pltpu.VMEM((slices, width, width), F32),
            pltpu.VMEM((slices, 128, 128), F32),
            pltpu.SemaphoreType.DMA((arrived.shape[0],)),
            pltpu.SemaphoreType.DMA,
            pltpu.SemaphoreType.DMA((width // 128,)),
        ],
        compiler_params=pltpu.CompilerParams(vmem_limit_bytes=VMEM_LIMIT),
    )(arrived, prior_gram)


def per_device(local_obs, global_obs, row_counts, owner_map, prior_factor):
    arc_dev = local_obs.shape[0]
    arc_groups = lax.axis_size("arc")
    col_groups = lax.axis_size("col")
    counts = lax.dynamic_slice_in_dim(row_counts, lax.axis_index("col") * arc_dev, arc_dev)
    order = jnp.arange(arc_dev, dtype=jnp.int32)
    dest = owner_map // SLICE_DEV // col_groups
    label = owner_map % SLICE_DEV
    earlier = (dest[None, :] == dest[:, None]) & (order[None, :] < order[:, None])
    slot = jnp.sum(earlier.astype(jnp.int32), axis=1)
    z, prior_gram = local_part(counts, local_obs, prior_factor)
    x = jnp.transpose(global_obs, (1, 2, 0))
    columns = []
    for h in range(CHUNKS):
        packed = layout(x, h, (z, dest, slot, label) if h else ())
        moved = lax.all_to_all(packed, "col", split_axis=0, concat_axis=0, tiled=True)
        columns.append(moved.reshape(col_groups, arc_dev, *packed.shape[1:]))
    kept = eliminate(dest, slot, label, columns, z, arc_groups)
    arrived = lax.all_to_all(kept, "arc", split_axis=0, concat_axis=0, tiled=True)
    return factor(arrived, prior_gram)


def solution(mesh):
    placed = (
        P(("arc", "col"), None, None),
        P("arc", None, "col"),
        P("arc"),
        P(("arc", "col")),
        P(("arc", "col"), None, None),
    )
    return jax.shard_map(
        per_device,
        mesh=mesh,
        in_specs=placed,
        out_specs=P(("arc", "col"), None, None),
        check_vma=False,
    )
```

```python
import functools

import jax
import jax.numpy as jnp
from jax import lax
from jax.experimental import pallas as pl
from jax.experimental.pallas import tpu as pltpu
from jax.sharding import PartitionSpec as P

SLICE_DEV = 2
HI = lax.Precision.HIGHEST
F32 = jnp.float32
BF16 = jnp.bfloat16
NN = (((1,), (0,)), ((), ()))
NT = (((1,), (1,)), ((), ()))
TN = (((0,), (0,)), ((), ()))
VMEM_LIMIT = 60 * 1024 * 1024


def dot(a, b, dims, precision=None):
    return lax.dot_general(a, b, dims, precision=precision, preferred_element_type=F32)


def split2(x):
    high = x.astype(BF16)
    return high, (x - high.astype(F32)).astype(BF16)


def dot3(a, b, dims):
    ah, al = a
    bh, bl = b
    ka, kb = dims[0][0][0], dims[0][1][0]
    left = jnp.concatenate([ah, ah, al], axis=ka)
    return dot(left, jnp.concatenate([bh, bl, bh], axis=kb), dims)


def split3(x):
    high = x.astype(BF16).astype(F32)
    rest = x - high
    mid = rest.astype(BF16).astype(F32)
    return high, mid, rest - mid


def outer6(left, right):
    lh, lm, ll = split3(left)
    rh, rm, rl = split3(right)
    a = jnp.concatenate([lh, lh, lm, lh, ll, lm], axis=0).astype(BF16)
    b = jnp.concatenate([rh, rm, rh, rl, rh, rm], axis=0).astype(BF16)
    return dot(a, b, TN)


def outer3(left, right):
    lh, lm, _ = split3(left)
    rh, rm, _ = split3(right)
    a = jnp.concatenate([lh, lh, left - lh], axis=0).astype(BF16)
    b = jnp.concatenate([rh, right - rh, rh], axis=0).astype(BF16)
    return dot(a, b, TN)


def row_of(x, i):
    return jnp.broadcast_to(x[:, i : i + 1, :], x.shape)


def lane_of(x, i):
    return jnp.broadcast_to(x[:, :, i : i + 1], x.shape)


def panel_rows(p):
    return pl.ds(pl.multiple_of(8 * p, 8), 8)


def places(x, p):
    lane = lax.broadcasted_iota(jnp.int32, x.shape, 2) - 8 * p
    return lane, lax.broadcasted_iota(jnp.int32, x.shape, 1)


def columns_of(x, p):
    turned = pltpu.roll(x, lax.rem(128 - 8 * p, 128), 2)
    return [lane_of(turned, l) for l in range(8)]


def batch_panel(x, following, p):
    lane, sub = places(x, p)
    inside = (lane >= 0) & (lane < 8)
    c = columns_of(x, p)
    n = columns_of(following, p)
    place = jnp.where(inside, (lane == sub).astype(F32), x)
    following = jnp.where(inside, 0.0, following)
    pivots = x
    for i in range(8):
        d = row_of(c[i], i)
        inv = pl.reciprocal(d, approx=True)
        pivots = jnp.where(sub == i, d, pivots)
        below = jnp.where(sub > i, c[i], 0.0)
        below_n = n[i]
        for l in range(i + 1, 8):
            r = row_of(c[l], i)
            c[l] = c[l] - (below * r) * inv
            n[l] = n[l] - (below_n * r) * inv
        below = below * inv
        r = row_of(place, i)
        place = place - below * r
        following = following - (below_n * inv) * r
    scale = lax.rsqrt(pivots)
    return place * scale, following


def cholesky_batch(a_ref):
    count = a_ref.shape[0]

    def step(p, carry):
        left, right, x = carry
        a = a_ref[...]
        at_lane, at_row = places(a, p)
        t = jnp.stack([outer6(left[b], right[b]) for b in range(count)], axis=0)
        cleared = (at_lane < 0) & (at_lane >= -8) & (at_row >= 8 * p + 8)
        a_ref[...] = jnp.where(cleared, 0.0, a) - t
        following = a_ref[:, panel_rows(jnp.minimum(p + 1, 15)), :]
        place, following = batch_panel(x, following, p)
        lane, sub = places(x, p)
        a_ref[:, panel_rows(p), :] = place
        return jnp.where(lane >= 16, place, 0.0), place, following

    first = a_ref[:, :8, :]
    lax.fori_loop(0, 16, step, (jnp.zeros_like(first), jnp.zeros_like(first), first))


def columns_at(x, p):
    return [lane_of(x, 8 * p + l) for l in range(8)]


def cholesky_panel(x, c, following, p):
    lane, sub = places(x, p)
    inside = (lane >= 0) & (lane < 8)
    c = list(c)
    place = jnp.where(inside, (lane == sub).astype(F32), x)
    n = ahead = None
    if following is not None:
        n = columns_at(following, p)
        ahead = columns_at(following, p + 1)
        following = jnp.where(inside, 0.0, following)
    upper = x
    pivots = x
    for i in range(8):
        d = row_of(c[i], i)
        inv = pl.reciprocal(d, approx=True)
        pivots = jnp.where(sub == i, d, pivots)
        below = jnp.where(sub > i, c[i], 0.0)
        for l in range(i + 1, 8):
            r = row_of(c[l], i) * inv
            c[l] = c[l] - below * r
            if n is not None:
                n[l] = n[l] - n[i] * r
        r = row_of(place, i) * inv
        place = place - below * r
        if n is not None:
            following = following - n[i] * r
            less = n[i] * inv
            ahead = [ahead[l] - less * row_of(n[i], l) for l in range(8)]
        upper = upper - below * (row_of(upper, i) * inv)
    scale = lax.rsqrt(pivots)
    return upper * scale, place * scale, following, ahead


def cholesky_blocks(a_ref, store_upper):
    count = a_ref.shape[0]
    rows = [a_ref[:, 8 * q : 8 * q + 8, :] for q in range(16)]
    c = columns_at(rows[0], 0)
    for p in range(16):
        following = rows[p + 1] if p < 15 else None
        upper, place, following, c = cholesky_panel(rows[p], c, following, p)
        lane, sub = places(place, p)
        inside = (lane >= 0) & (lane < 8)
        a_ref[:, 8 * p : 8 * p + 8, :] = place
        if store_upper is not None:
            store_upper(p, jnp.where(lane >= sub, upper, 0.0))
        if p < 15:
            rows[p + 1] = following
        if p < 14:
            left = jnp.where(lane >= 16, place, 0.0)
            t = [outer3(left[b], place[b]) for b in range(count)]
            for q in range(p + 2, 16):
                part = jnp.stack([v[8 * q : 8 * q + 8] for v in t], axis=0)
                rows[q] = jnp.where(inside, 0.0, rows[q]) - part


def inverse_panel(a_ref, sign_ref, p):
    x = a_ref[:, panel_rows(p), :]
    lane, sub = places(x, p)
    c = columns_of(x, p)
    place = jnp.where((lane >= 0) & (lane < 8), (lane == sub).astype(F32), x)
    signs = sign_ref[...]
    for i in range(8):
        pv = row_of(c[i], i)
        s = jnp.where(pv >= 0.0, -1.0, 1.0)
        signs = jnp.where(lane == i, s, signs)
        inv = pl.reciprocal(pv - s, approx=True)
        lm = jnp.where(sub == i, 1.0 - inv, c[i] * inv)
        for l in range(i + 1, 8):
            c[l] = c[l] - lm * row_of(c[l], i)
        place = place - lm * row_of(place, i)
    sign_ref[...] = signs
    a = a_ref[...]
    at_lane, at_row = places(a, p)
    wide = jnp.concatenate([place] * 16, axis=1)
    factor = jnp.where((at_row >= 8 * p) & (at_row < 8 * p + 8), wide, 0.0)
    t = jnp.stack([dot(a[b], factor[b], NN, HI) for b in range(x.shape[0])], axis=0)
    a_ref[...] = jnp.where((at_lane >= 0) & (at_lane < 8), 0.0, a) - t
    a_ref[:, panel_rows(p), :] = place


def layout_kernel(x_ref, o_ref, x_buf, o_buf, in_sems, out_sems):
    rows, cols, arcs = x_ref.shape
    blocks = cols // 8
    arriving = []
    for b in range(blocks):
        copy = pltpu.make_async_copy(x_ref.at[:, 8 * b : 8 * b + 8, :], x_buf.at[b], in_sems.at[b])
        copy.start()
        arriving.append(copy)
    leaving = []

    def put(row, tiles):
        o_buf[:, row : row + 8, :] = jnp.transpose(tiles, (1, 0, 2))
        where = slice(row, row + 8)
        copy = pltpu.make_async_copy(o_buf.at[:, where, :], o_ref.at[:, where, :], out_sems.at[len(leaving)])
        copy.start()
        leaving.append(copy)

    ends = []
    for b in range(blocks):
        arriving[b].wait()
        for tile in range(2):
            v = jnp.transpose(x_buf[b, 128 * tile : 128 * tile + 128], (1, 0, 2))
            put(tile * cols + 8 * b, jnp.stack([v[c].T for c in range(8)], axis=0))
        ends.append(jnp.transpose(x_buf[b, 256:], (1, 0, 2)))
        if b % 2:
            both = jnp.concatenate(ends, axis=1)
            put(2 * cols + 4 * (b - 1), jnp.stack([both[c].T for c in range(8)], axis=0))
            ends = []
    for copy in leaving:
        copy.wait()


def layout(x):
    rows, cols, arcs = x.shape
    packed = 2 * cols + cols // 2
    hbm = pl.BlockSpec(memory_space=pltpu.HBM)
    return pl.pallas_call(
        layout_kernel,
        out_shape=jax.ShapeDtypeStruct((arcs, packed, 128), F32),
        in_specs=[hbm],
        out_specs=hbm,
        scratch_shapes=[
            pltpu.VMEM((cols // 8, rows, 8, arcs), F32),
            pltpu.VMEM((arcs, packed, 128), F32),
            pltpu.SemaphoreType.DMA((cols // 8,)),
            pltpu.SemaphoreType.DMA((packed // 8,)),
        ],
        compiler_params=pltpu.CompilerParams(vmem_limit_bytes=VMEM_LIMIT),
    )(x)


def local_kernel(counts_ref, l_ref, prior_ref, z_ref, info_ref, a_ref, q_ref, sign_ref):
    arcs, rows, loc = l_ref.shape
    place = lax.broadcasted_iota(jnp.int32, (rows, loc), 0)
    for b in range(arcs):
        masked = jnp.where(place < counts_ref[b], l_ref[b], 0.0)
        q_ref[b] = masked
        a_ref[b] = dot(masked, masked, TN, HI)
    cholesky_batch(a_ref)
    r = lax.broadcasted_iota(jnp.int32, (loc, loc), 0)
    l = lax.broadcasted_iota(jnp.int32, (loc, loc), 1)
    for b in range(arcs):
        basis = dot(q_ref[b], jnp.where(l <= r, a_ref[b], 0.0), NT, HI)
        q_ref[b] = basis
        a_ref[b] = basis[:loc]
    sign_ref[...] = jnp.zeros_like(sign_ref)

    def invert(p, carry):
        inverse_panel(a_ref, sign_ref, p)
        return carry

    lax.fori_loop(0, loc // 8, invert, 0)
    rest = rows - loc
    unit = (place == lax.broadcasted_iota(jnp.int32, (rows, loc), 1)).astype(F32)
    r2 = lax.broadcasted_iota(jnp.int32, (rest, rows), 0)
    l2 = lax.broadcasted_iota(jnp.int32, (rest, rows), 1)
    for b in range(arcs):
        q = q_ref[b]
        n = dot(q[loc:], a_ref[b], NN, HI)
        v = q * sign_ref[b][0:1] - unit
        keep = (l2 == r2 + loc) & (l2 < counts_ref[b])
        z = dot(n, v, NT, HI) + keep.astype(F32)
        zh, zl = split2(jnp.concatenate([z, z[:, 256:]], axis=1))
        z_ref[b, 0] = zh
        z_ref[b, 1] = zl
    half = prior_ref.shape[1] // 2
    for s in range(prior_ref.shape[0]):
        top = prior_ref[s, :half, :]
        low = prior_ref[s, :, half:]
        info_ref[s, :half, :] = dot(top[:, :half], top, TN, HI)
        info_ref[s, half:, half:] = dot(low, low, TN, HI)
        info_ref[s, half:, :half] = jnp.zeros((half, half), F32)


def local_part(counts, local_obs, prior):
    arcs, rows, loc = local_obs.shape
    vmem = pl.BlockSpec(memory_space=pltpu.VMEM)
    return pl.pallas_call(
        local_kernel,
        out_shape=(
            jax.ShapeDtypeStruct((arcs, 2, rows - loc, 384), BF16),
            jax.ShapeDtypeStruct(prior.shape, F32),
        ),
        in_specs=[pl.BlockSpec(memory_space=pltpu.SMEM), vmem, vmem],
        out_specs=(vmem, vmem),
        scratch_shapes=[
            pltpu.VMEM((arcs, loc, loc), F32),
            pltpu.VMEM((arcs, rows, loc), F32),
            pltpu.VMEM((arcs, 8, loc), F32),
        ],
        compiler_params=pltpu.CompilerParams(vmem_limit_bytes=VMEM_LIMIT),
    )(counts, local_obs, prior)


def eliminate_kernel(
    dest_ref, slot_ref, label_ref, g_hbm, z_hbm, o_ref, g_buf, z_buf, main_ref, tail_ref, g_sems, z_sems, sems, tail_sem
):
    arcs, sources, packed, _ = g_buf.shape
    part = packed * 2 // 5
    width = sources * part

    def columns(a):
        return pltpu.make_async_copy(g_hbm.at[:, a], g_buf.at[a], g_sems.at[a])

    def weights(a):
        return pltpu.make_async_copy(z_hbm.at[a], z_buf.at[a], z_sems.at[a])

    for a in range(arcs):
        columns(a).start()
        weights(a).start()
    tail_ref[...] = jnp.zeros_like(tail_ref)
    tail_ref[:, width:, :] = jnp.full((tail_ref.shape[0], 8, 128), -1.0, F32)

    def reduced(a):
        g = [g_buf[a, :, i * part : (i + 1) * part, :].reshape(width, 128) for i in range(2)]
        t = g_buf[a, :, 2 * part :, :].reshape(width // 16, 8, 128)
        first = lax.broadcasted_iota(jnp.int32, t.shape, 2) < 64
        ends = jnp.stack([jnp.where(own, t, 0.0) for own in (first, ~first)], axis=1).reshape(width, 128)
        zh, zl = [jnp.concatenate([z_buf[a, i], jnp.zeros((64, 384), BF16)], axis=0) for i in range(2)]
        return dot3(split2(jnp.concatenate([*g, ends], axis=1)), (zh, zl), NT)

    def pair(i, carry):
        both = (2 * i, 2 * i + 1)
        for a in both:
            columns(a).wait()
            weights(a).wait()
        results = [reduced(a) for a in both]
        for a, r in zip(both, results):
            slot = slot_ref[a]
            dest = dest_ref[a]
            main_ref[a] = r[:, :128]
            rows = pl.ds(pl.multiple_of(width * slot, 8), width)
            pltpu.make_async_copy(main_ref.at[a], o_ref.at[dest, rows, :], sems.at[a]).start()
            tail_ref[dest, :width, :] += pltpu.roll(r[:, 128:], 64 * slot, 1)
            labels = tail_ref[dest, width:, :]
            at = lax.broadcasted_iota(jnp.int32, labels.shape, 0)
            tail_ref[dest, width:, :] = jnp.where(at == slot, label_ref[a].astype(F32), labels)
        return carry

    lax.fori_loop(0, arcs // 2, pair, 0)
    ends_copy = pltpu.make_async_copy(tail_ref, o_ref.at[:, 2 * width :, :], tail_sem)
    ends_copy.start()
    for a in range(arcs):
        pltpu.make_async_copy(main_ref.at[a], o_ref.at[0, :width, :], sems.at[a]).wait()
    ends_copy.wait()


def eliminate(dest, slot, label, g, z, groups):
    sources, arcs, packed, _ = g.shape
    width = sources * packed * 2 // 5
    smem = pl.BlockSpec(memory_space=pltpu.SMEM)
    hbm = pl.BlockSpec(memory_space=pltpu.HBM)
    return pl.pallas_call(
        eliminate_kernel,
        out_shape=jax.ShapeDtypeStruct((groups, 3 * width + 8, 128), F32),
        in_specs=[smem, smem, smem, hbm, hbm],
        out_specs=hbm,
        scratch_shapes=[
            pltpu.VMEM((arcs, sources, packed, 128), F32),
            pltpu.VMEM(z.shape, BF16),
            pltpu.VMEM((arcs, width, 128), F32),
            pltpu.VMEM((groups, width + 8, 128), F32),
            pltpu.SemaphoreType.DMA((arcs,)),
            pltpu.SemaphoreType.DMA((arcs,)),
            pltpu.SemaphoreType.DMA((arcs,)),
            pltpu.SemaphoreType.DMA,
        ],
        compiler_params=pltpu.CompilerParams(vmem_limit_bytes=VMEM_LIMIT),
    )(dest, slot, label, g, z)


def factor_kernel(x_hbm, prior_ref, out_hbm, list_ref, x_buf, info_ref, out_ref, a_ref, sems, prior_sem, out_sems):
    slices, width, _ = info_ref.shape
    groups = x_buf.shape[0] - 1
    half = width // 2

    def rows_of(n):
        return pltpu.make_async_copy(x_hbm.at[n], x_buf.at[n], sems.at[n])

    start = pltpu.make_async_copy(prior_ref, info_ref, prior_sem)
    start.start()
    for n in range(groups):
        rows_of(n).start()
    x_buf[groups] = jnp.zeros_like(x_buf[groups])
    start.wait()

    def listed(n, count):
        rows_of(n).wait()
        labels = x_buf[n, 3 * width :, :]
        for slot in range(2):
            label = labels[slot, 0].astype(jnp.int32)
            list_ref[0, count] = n
            list_ref[1, count] = slot
            list_ref[2, count] = label
            count = count + (label >= 0).astype(jnp.int32)
        return count

    count = lax.fori_loop(0, groups, listed, 0)
    list_ref[0, count] = groups
    list_ref[1, count] = 0
    list_ref[2, count] = 0

    def add(pair, carry):
        items = []
        for i in range(2):
            n, slot = list_ref[0, 2 * pair + i], list_ref[1, 2 * pair + i]
            main = x_buf[n, pl.ds(pl.multiple_of(slot * width, 8), width), :]
            tail = x_buf[n, 2 * width : 3 * width, :]
            own = lax.broadcasted_iota(jnp.int32, tail.shape, 1) // 64 == slot
            h, l = split2(jnp.concatenate([main, jnp.where(own, tail, 0.0)], axis=1))
            top = dot3((h[:half], l[:half]), (h, l), NT)
            items.append((list_ref[2, 2 * pair + i], top, dot3((h[half:], l[half:]), (h[half:], l[half:]), NT)))
        for label, top, low in items:
            info_ref[label, :half, :] += top
            info_ref[label, half:, half:] += low
        return carry

    lax.fori_loop(0, (count + 1) // 2, add, 0)
    r = lax.broadcasted_iota(jnp.int32, (128, 128), 0)
    l = lax.broadcasted_iota(jnp.int32, (128, 128), 1)
    leaving = []
    for k in range(width // 128):
        lo, hi = 128 * k, 128 * k + 128
        block = a_ref.at[k % 2]
        block[...] = info_ref[:, lo:hi, lo:hi]
        if k:
            out_ref[:, lo:hi, :lo] = jnp.zeros((slices, 128, lo), F32)

        def store(p, rows):
            out_ref[:, lo + 8 * p : lo + 8 * p + 8, lo:hi] = rows

        cholesky_blocks(block, store)
        inverses = [split2(jnp.where(l <= r, block[s], 0.0)) for s in range(slices)]
        right = [[None] * slices for _ in range(width // 128)]
        for j in range(k + 1, width // 128):
            for s in range(slices):
                u = dot3(inverses[s], split2(info_ref[s, lo:hi, 128 * j : 128 * j + 128]), NN)
                out_ref[s, lo:hi, 128 * j : 128 * j + 128] = u
                right[j][s] = split2(u)
            for i in range(k + 1, j + 1):
                for s in range(slices):
                    less = dot3(right[i][s], right[j][s], TN)
                    info_ref[s, 128 * i : 128 * i + 128, 128 * j : 128 * j + 128] -= less
        copy = pltpu.make_async_copy(out_ref.at[:, lo:hi, :], out_hbm.at[:, lo:hi, :], out_sems.at[k])
        copy.start()
        leaving.append(copy)
    for copy in leaving:
        copy.wait()


def factor(arrived, prior_gram):
    slices, width, _ = prior_gram.shape
    hbm = pl.BlockSpec(memory_space=pltpu.HBM)
    return pl.pallas_call(
        factor_kernel,
        out_shape=jax.ShapeDtypeStruct(prior_gram.shape, F32),
        in_specs=[hbm, pl.BlockSpec(memory_space=pl.ANY)],
        out_specs=hbm,
        scratch_shapes=[
            pltpu.SMEM((3, 2 * arrived.shape[0] + 1), jnp.int32),
            pltpu.VMEM((arrived.shape[0] + 1, *arrived.shape[1:]), F32),
            pltpu.VMEM((slices, width, width), F32),
            pltpu.VMEM((slices, width, width), F32),
            pltpu.VMEM((2, slices, 128, 128), F32),
            pltpu.SemaphoreType.DMA((arrived.shape[0],)),
            pltpu.SemaphoreType.DMA,
            pltpu.SemaphoreType.DMA((width // 128,)),
        ],
        compiler_params=pltpu.CompilerParams(vmem_limit_bytes=VMEM_LIMIT),
    )(arrived, prior_gram)


def per_device(local_obs, global_obs, row_counts, owner_map, prior_factor):
    arc_dev = local_obs.shape[0]
    arc_groups = lax.axis_size("arc")
    col_groups = lax.axis_size("col")
    counts = lax.dynamic_slice_in_dim(row_counts, lax.axis_index("col") * arc_dev, arc_dev)
    packed = layout(jnp.transpose(global_obs, (1, 2, 0)))
    columns = lax.all_to_all(packed, "col", split_axis=0, concat_axis=0, tiled=True)
    columns = columns.reshape(col_groups, arc_dev, *packed.shape[1:])
    order = jnp.arange(arc_dev, dtype=jnp.int32)
    dest = owner_map // SLICE_DEV // col_groups
    earlier = (dest[None, :] == dest[:, None]) & (order[None, :] < order[:, None])
    slot = jnp.sum(earlier.astype(jnp.int32), axis=1)
    z, prior_gram = local_part(counts, local_obs, prior_factor)
    kept = eliminate(dest, slot, owner_map % SLICE_DEV, columns, z, arc_groups)
    arrived = lax.all_to_all(kept, "arc", split_axis=0, concat_axis=0, tiled=True)
    return factor(arrived, prior_gram)


def solution(mesh):
    placed = (
        P(("arc", "col"), None, None),
        P("arc", None, "col"),
        P("arc"),
        P(("arc", "col")),
        P(("arc", "col"), None, None),
    )
    return jax.shard_map(
        per_device,
        mesh=mesh,
        in_specs=placed,
        out_specs=P(("arc", "col"), None, None),
        check_vma=False,
    )
```

```python
import functools

import jax
import jax.numpy as jnp
from jax import lax
from jax.experimental import pallas as pl
from jax.experimental.pallas import tpu as pltpu
from jax.sharding import PartitionSpec as P

SLICE_DEV = 2
HI = lax.Precision.HIGHEST
F32 = jnp.float32
BF16 = jnp.bfloat16
NN = (((1,), (0,)), ((), ()))
NT = (((1,), (1,)), ((), ()))
TN = (((0,), (0,)), ((), ()))
VMEM_LIMIT = 60 * 1024 * 1024


def dot(a, b, dims, precision=None):
    return lax.dot_general(a, b, dims, precision=precision, preferred_element_type=F32)


def split2(x):
    high = x.astype(BF16)
    return high, (x - high.astype(F32)).astype(BF16)


def dot3(a, b, dims):
    ah, al = a
    bh, bl = b
    ka, kb = dims[0][0][0], dims[0][1][0]
    left = jnp.concatenate([ah, ah, al], axis=ka)
    return dot(left, jnp.concatenate([bh, bl, bh], axis=kb), dims)


def split3(x):
    high = x.astype(BF16).astype(F32)
    rest = x - high
    mid = rest.astype(BF16).astype(F32)
    return high, mid, rest - mid


def outer6(left, right):
    lh, lm, ll = split3(left)
    rh, rm, rl = split3(right)
    a = jnp.concatenate([lh, lh, lm, lh, ll, lm], axis=0).astype(BF16)
    b = jnp.concatenate([rh, rm, rh, rl, rh, rm], axis=0).astype(BF16)
    return dot(a, b, TN)


def outer3(left, right):
    lh, lm, _ = split3(left)
    rh, rm, _ = split3(right)
    a = jnp.concatenate([lh, lh, left - lh], axis=0).astype(BF16)
    b = jnp.concatenate([rh, right - rh, rh], axis=0).astype(BF16)
    return dot(a, b, TN)


def row_of(x, i):
    return jnp.broadcast_to(x[:, i : i + 1, :], x.shape)


def lane_of(x, i):
    return jnp.broadcast_to(x[:, :, i : i + 1], x.shape)


def panel_rows(p):
    return pl.ds(pl.multiple_of(8 * p, 8), 8)


def places(x, p):
    lane = lax.broadcasted_iota(jnp.int32, x.shape, 2) - 8 * p
    return lane, lax.broadcasted_iota(jnp.int32, x.shape, 1)


def columns_of(x, p):
    turned = pltpu.roll(x, lax.rem(128 - 8 * p, 128), 2)
    return [lane_of(turned, l) for l in range(8)]


def batch_panel(x, following, p):
    lane, sub = places(x, p)
    inside = (lane >= 0) & (lane < 8)
    c = columns_of(x, p)
    n = columns_of(following, p)
    place = jnp.where(inside, (lane == sub).astype(F32), x)
    following = jnp.where(inside, 0.0, following)
    pivots = x
    for i in range(8):
        d = row_of(c[i], i)
        inv = pl.reciprocal(d, approx=True)
        pivots = jnp.where(sub == i, d, pivots)
        below = jnp.where(sub > i, c[i], 0.0)
        below_n = n[i]
        for l in range(i + 1, 8):
            r = row_of(c[l], i)
            c[l] = c[l] - (below * r) * inv
            n[l] = n[l] - (below_n * r) * inv
        below = below * inv
        r = row_of(place, i)
        place = place - below * r
        following = following - (below_n * inv) * r
    scale = lax.rsqrt(pivots)
    return place * scale, following


def cholesky_batch(a_ref):
    count = a_ref.shape[0]

    def step(p, carry):
        left, right, x = carry
        a = a_ref[...]
        at_lane, at_row = places(a, p)
        t = jnp.stack([outer6(left[b], right[b]) for b in range(count)], axis=0)
        cleared = (at_lane < 0) & (at_lane >= -8) & (at_row >= 8 * p + 8)
        a_ref[...] = jnp.where(cleared, 0.0, a) - t
        following = a_ref[:, panel_rows(jnp.minimum(p + 1, 15)), :]
        place, following = batch_panel(x, following, p)
        lane, sub = places(x, p)
        a_ref[:, panel_rows(p), :] = place
        return jnp.where(lane >= 16, place, 0.0), place, following

    first = a_ref[:, :8, :]
    lax.fori_loop(0, 16, step, (jnp.zeros_like(first), jnp.zeros_like(first), first))


def columns_at(x, p):
    return [lane_of(x, 8 * p + l) for l in range(8)]


def cholesky_panel(x, c, following, p):
    lane, sub = places(x, p)
    inside = (lane >= 0) & (lane < 8)
    c = list(c)
    place = jnp.where(inside, (lane == sub).astype(F32), x)
    n = ahead = None
    if following is not None:
        n = columns_at(following, p)
        ahead = columns_at(following, p + 1)
        following = jnp.where(inside, 0.0, following)
    upper = x
    pivots = x
    for i in range(8):
        d = row_of(c[i], i)
        inv = pl.reciprocal(d, approx=True)
        pivots = jnp.where(sub == i, d, pivots)
        below = jnp.where(sub > i, c[i], 0.0)
        for l in range(i + 1, 8):
            r = row_of(c[l], i) * inv
            c[l] = c[l] - below * r
            if n is not None:
                n[l] = n[l] - n[i] * r
        r = row_of(place, i) * inv
        place = place - below * r
        if n is not None:
            following = following - n[i] * r
            less = n[i] * inv
            ahead = [ahead[l] - less * row_of(n[i], l) for l in range(8)]
        upper = upper - below * (row_of(upper, i) * inv)
    scale = lax.rsqrt(pivots)
    return upper * scale, place * scale, following, ahead


def cholesky_blocks(a_ref, store_upper):
    count = a_ref.shape[0]
    rows = [a_ref[:, 8 * q : 8 * q + 8, :] for q in range(16)]
    c = columns_at(rows[0], 0)
    for p in range(16):
        following = rows[p + 1] if p < 15 else None
        upper, place, following, c = cholesky_panel(rows[p], c, following, p)
        lane, sub = places(place, p)
        inside = (lane >= 0) & (lane < 8)
        a_ref[:, 8 * p : 8 * p + 8, :] = place
        if store_upper is not None:
            store_upper(p, jnp.where(lane >= sub, upper, 0.0))
        if p < 15:
            rows[p + 1] = following
        if p < 14:
            left = jnp.where(lane >= 16, place, 0.0)
            t = [outer3(left[b], place[b]) for b in range(count)]
            for q in range(p + 2, 16):
                part = jnp.stack([v[8 * q : 8 * q + 8] for v in t], axis=0)
                rows[q] = jnp.where(inside, 0.0, rows[q]) - part


def inverse_panel(a_ref, sign_ref, p):
    x = a_ref[:, panel_rows(p), :]
    lane, sub = places(x, p)
    c = columns_of(x, p)
    place = jnp.where((lane >= 0) & (lane < 8), (lane == sub).astype(F32), x)
    signs = sign_ref[...]
    for i in range(8):
        pv = row_of(c[i], i)
        s = jnp.where(pv >= 0.0, -1.0, 1.0)
        signs = jnp.where(lane == i, s, signs)
        inv = pl.reciprocal(pv - s, approx=True)
        lm = jnp.where(sub == i, 1.0 - inv, c[i] * inv)
        for l in range(i + 1, 8):
            c[l] = c[l] - lm * row_of(c[l], i)
        place = place - lm * row_of(place, i)
    sign_ref[...] = signs
    a = a_ref[...]
    at_lane, at_row = places(a, p)
    wide = jnp.concatenate([place] * 16, axis=1)
    factor = jnp.where((at_row >= 8 * p) & (at_row < 8 * p + 8), wide, 0.0)
    t = jnp.stack([dot(a[b], factor[b], NN, HI) for b in range(x.shape[0])], axis=0)
    a_ref[...] = jnp.where((at_lane >= 0) & (at_lane < 8), 0.0, a) - t
    a_ref[:, panel_rows(p), :] = place


def layout_kernel(x_ref, o_ref, x_buf, o_buf, in_sems, out_sems):
    rows, cols, arcs = x_ref.shape
    blocks = cols // 8
    arriving = []
    for b in range(blocks):
        copy = pltpu.make_async_copy(x_ref.at[:, 8 * b : 8 * b + 8, :], x_buf.at[b], in_sems.at[b])
        copy.start()
        arriving.append(copy)
    leaving = []

    def put(row, tiles):
        o_buf[:, row : row + 8, :] = jnp.transpose(tiles, (1, 0, 2))
        where = slice(row, row + 8)
        copy = pltpu.make_async_copy(o_buf.at[:, where, :], o_ref.at[:, where, :], out_sems.at[len(leaving)])
        copy.start()
        leaving.append(copy)

    ends = []
    for b in range(blocks):
        arriving[b].wait()
        for tile in range(2):
            v = jnp.transpose(x_buf[b, 128 * tile : 128 * tile + 128], (1, 0, 2))
            put(tile * cols + 8 * b, jnp.stack([v[c].T for c in range(8)], axis=0))
        ends.append(jnp.transpose(x_buf[b, 256:], (1, 0, 2)))
        if b % 2:
            both = jnp.concatenate(ends, axis=1)
            put(2 * cols + 4 * (b - 1), jnp.stack([both[c].T for c in range(8)], axis=0))
            ends = []
    for copy in leaving:
        copy.wait()


def layout(x):
    rows, cols, arcs = x.shape
    packed = 2 * cols + cols // 2
    hbm = pl.BlockSpec(memory_space=pltpu.HBM)
    return pl.pallas_call(
        layout_kernel,
        out_shape=jax.ShapeDtypeStruct((arcs, packed, 128), F32),
        in_specs=[hbm],
        out_specs=hbm,
        scratch_shapes=[
            pltpu.VMEM((cols // 8, rows, 8, arcs), F32),
            pltpu.VMEM((arcs, packed, 128), F32),
            pltpu.SemaphoreType.DMA((cols // 8,)),
            pltpu.SemaphoreType.DMA((packed // 8,)),
        ],
        compiler_params=pltpu.CompilerParams(vmem_limit_bytes=VMEM_LIMIT),
    )(x)


def local_kernel(counts_ref, l_ref, prior_ref, z_ref, info_ref, a_ref, q_ref, sign_ref):
    arcs, rows, loc = l_ref.shape
    place = lax.broadcasted_iota(jnp.int32, (rows, loc), 0)
    for b in range(arcs):
        masked = jnp.where(place < counts_ref[b], l_ref[b], 0.0)
        q_ref[b] = masked
        a_ref[b] = dot(masked, masked, TN, HI)
    cholesky_batch(a_ref)
    r = lax.broadcasted_iota(jnp.int32, (loc, loc), 0)
    l = lax.broadcasted_iota(jnp.int32, (loc, loc), 1)
    for b in range(arcs):
        basis = dot(q_ref[b], jnp.where(l <= r, a_ref[b], 0.0), NT, HI)
        q_ref[b] = basis
        a_ref[b] = basis[:loc]
    sign_ref[...] = jnp.zeros_like(sign_ref)

    def invert(p, carry):
        inverse_panel(a_ref, sign_ref, p)
        return carry

    lax.fori_loop(0, loc // 8, invert, 0)
    rest = rows - loc
    unit = (place == lax.broadcasted_iota(jnp.int32, (rows, loc), 1)).astype(F32)
    r2 = lax.broadcasted_iota(jnp.int32, (rest, rows), 0)
    l2 = lax.broadcasted_iota(jnp.int32, (rest, rows), 1)
    for b in range(arcs):
        q = q_ref[b]
        n = dot(q[loc:], a_ref[b], NN, HI)
        v = q * sign_ref[b][0:1] - unit
        keep = (l2 == r2 + loc) & (l2 < counts_ref[b])
        z = dot(n, v, NT, HI) + keep.astype(F32)
        zh, zl = split2(jnp.concatenate([z, z[:, 256:]], axis=1))
        z_ref[b, 0] = zh
        z_ref[b, 1] = zl
    half = prior_ref.shape[1] // 2
    for s in range(prior_ref.shape[0]):
        top = prior_ref[s, :half, :]
        low = prior_ref[s, :, half:]
        info_ref[s, :half, :] = dot(top[:, :half], top, TN, HI)
        info_ref[s, half:, half:] = dot(low, low, TN, HI)
        info_ref[s, half:, :half] = jnp.zeros((half, half), F32)


def local_part(counts, local_obs, prior):
    arcs, rows, loc = local_obs.shape
    vmem = pl.BlockSpec(memory_space=pltpu.VMEM)
    return pl.pallas_call(
        local_kernel,
        out_shape=(
            jax.ShapeDtypeStruct((arcs, 2, rows - loc, 384), BF16),
            jax.ShapeDtypeStruct(prior.shape, F32),
        ),
        in_specs=[pl.BlockSpec(memory_space=pltpu.SMEM), vmem, vmem],
        out_specs=(vmem, vmem),
        scratch_shapes=[
            pltpu.VMEM((arcs, loc, loc), F32),
            pltpu.VMEM((arcs, rows, loc), F32),
            pltpu.VMEM((arcs, 8, loc), F32),
        ],
        compiler_params=pltpu.CompilerParams(vmem_limit_bytes=VMEM_LIMIT),
    )(counts, local_obs, prior)


def eliminate_kernel(
    dest_ref, slot_ref, label_ref, g_hbm, z_hbm, o_ref, g_buf, z_buf, main_ref, tail_ref, g_sems, z_sems, sems, tail_sem
):
    arcs, sources, packed, _ = g_buf.shape
    part = packed * 2 // 5
    width = sources * part

    def columns(a):
        return pltpu.make_async_copy(g_hbm.at[:, a], g_buf.at[a], g_sems.at[a])

    def weights(a):
        return pltpu.make_async_copy(z_hbm.at[a], z_buf.at[a], z_sems.at[a])

    for a in range(arcs):
        columns(a).start()
        weights(a).start()
    tail_ref[...] = jnp.zeros_like(tail_ref)
    tail_ref[:, width:, :] = jnp.full((tail_ref.shape[0], 8, 128), -1.0, F32)

    def reduced(a):
        g = [g_buf[a, :, i * part : (i + 1) * part, :].reshape(width, 128) for i in range(2)]
        t = g_buf[a, :, 2 * part :, :].reshape(width // 16, 8, 128)
        first = lax.broadcasted_iota(jnp.int32, t.shape, 2) < 64
        ends = jnp.stack([jnp.where(own, t, 0.0) for own in (first, ~first)], axis=1).reshape(width, 128)
        zh, zl = [jnp.concatenate([z_buf[a, i], jnp.zeros((64, 384), BF16)], axis=0) for i in range(2)]
        return dot3(split2(jnp.concatenate([*g, ends], axis=1)), (zh, zl), NT)

    def pair(i, carry):
        both = (2 * i, 2 * i + 1)
        for a in both:
            columns(a).wait()
            weights(a).wait()
        results = [reduced(a) for a in both]
        for a, r in zip(both, results):
            slot = slot_ref[a]
            dest = dest_ref[a]
            main_ref[a] = r[:, :128]
            rows = pl.ds(pl.multiple_of(width * slot, 8), width)
            pltpu.make_async_copy(main_ref.at[a], o_ref.at[dest, rows, :], sems.at[a]).start()
            tail_ref[dest, :width, :] += pltpu.roll(r[:, 128:], 64 * slot, 1)
            labels = tail_ref[dest, width:, :]
            at = lax.broadcasted_iota(jnp.int32, labels.shape, 0)
            tail_ref[dest, width:, :] = jnp.where(at == slot, label_ref[a].astype(F32), labels)
        return carry

    lax.fori_loop(0, arcs // 2, pair, 0)
    ends_copy = pltpu.make_async_copy(tail_ref, o_ref.at[:, 2 * width :, :], tail_sem)
    ends_copy.start()
    for a in range(arcs):
        pltpu.make_async_copy(main_ref.at[a], o_ref.at[0, :width, :], sems.at[a]).wait()
    ends_copy.wait()


def eliminate(dest, slot, label, g, z, groups):
    sources, arcs, packed, _ = g.shape
    width = sources * packed * 2 // 5
    smem = pl.BlockSpec(memory_space=pltpu.SMEM)
    hbm = pl.BlockSpec(memory_space=pltpu.HBM)
    return pl.pallas_call(
        eliminate_kernel,
        out_shape=jax.ShapeDtypeStruct((groups, 3 * width + 8, 128), F32),
        in_specs=[smem, smem, smem, hbm, hbm],
        out_specs=hbm,
        scratch_shapes=[
            pltpu.VMEM((arcs, sources, packed, 128), F32),
            pltpu.VMEM(z.shape, BF16),
            pltpu.VMEM((arcs, width, 128), F32),
            pltpu.VMEM((groups, width + 8, 128), F32),
            pltpu.SemaphoreType.DMA((arcs,)),
            pltpu.SemaphoreType.DMA((arcs,)),
            pltpu.SemaphoreType.DMA((arcs,)),
            pltpu.SemaphoreType.DMA,
        ],
        compiler_params=pltpu.CompilerParams(vmem_limit_bytes=VMEM_LIMIT),
    )(dest, slot, label, g, z)


def factor_kernel(
    x_hbm, prior_ref, out_hbm, list_ref, label_buf, x_buf, info_ref, out_ref, a_ref, sems, label_sem, prior_sem, out_sems
):
    slices, width, _ = info_ref.shape
    groups = x_buf.shape[0] - 1
    half = width // 2

    def rows_of(n):
        return pltpu.make_async_copy(x_hbm.at[n, : 3 * width, :], x_buf.at[n], sems.at[n])

    marks = pltpu.make_async_copy(x_hbm.at[:, 3 * width :, :], label_buf, label_sem)
    marks.start()
    start = pltpu.make_async_copy(prior_ref, info_ref, prior_sem)
    start.start()
    for n in range(groups):
        rows_of(n).start()
    x_buf[groups] = jnp.zeros_like(x_buf[groups])
    marks.wait()

    def listed(n, count):
        labels = label_buf[n]
        for slot in range(2):
            label = labels[slot, 0].astype(jnp.int32)
            list_ref[0, count] = n
            list_ref[1, count] = slot
            list_ref[2, count] = label
            count = count + (label >= 0).astype(jnp.int32)
        return count

    count = lax.fori_loop(0, groups, listed, 0)
    list_ref[0, count] = groups
    list_ref[1, count] = 0
    list_ref[2, count] = 0
    start.wait()

    def wait(n, carry):
        rows_of(n).wait()
        return carry

    def add(pair, ready):
        items = []
        needed = jnp.minimum(jnp.maximum(list_ref[0, 2 * pair], list_ref[0, 2 * pair + 1]) + 1, groups)
        lax.fori_loop(ready, needed, wait, 0)
        for i in range(2):
            n, slot = list_ref[0, 2 * pair + i], list_ref[1, 2 * pair + i]
            main = x_buf[n, pl.ds(pl.multiple_of(slot * width, 8), width), :]
            tail = x_buf[n, 2 * width : 3 * width, :]
            own = lax.broadcasted_iota(jnp.int32, tail.shape, 1) // 64 == slot
            h, l = split2(jnp.concatenate([main, jnp.where(own, tail, 0.0)], axis=1))
            top = dot3((h[:half], l[:half]), (h, l), NT)
            items.append((list_ref[2, 2 * pair + i], top, dot3((h[half:], l[half:]), (h[half:], l[half:]), NT)))
        for label, top, low in items:
            info_ref[label, :half, :] += top
            info_ref[label, half:, half:] += low
        return jnp.maximum(ready, needed)

    ready = lax.fori_loop(0, (count + 1) // 2, add, 0)
    lax.fori_loop(ready, groups, wait, 0)
    r = lax.broadcasted_iota(jnp.int32, (128, 128), 0)
    l = lax.broadcasted_iota(jnp.int32, (128, 128), 1)
    leaving = []
    for k in range(width // 128):
        lo, hi = 128 * k, 128 * k + 128
        block = a_ref.at[k % 2]
        block[...] = info_ref[:, lo:hi, lo:hi]
        if k:
            out_ref[:, lo:hi, :lo] = jnp.zeros((slices, 128, lo), F32)

        def store(p, rows):
            out_ref[:, lo + 8 * p : lo + 8 * p + 8, lo:hi] = rows

        cholesky_blocks(block, store)
        inverses = [split2(jnp.where(l <= r, block[s], 0.0)) for s in range(slices)]
        right = [[None] * slices for _ in range(width // 128)]
        for j in range(k + 1, width // 128):
            for s in range(slices):
                u = dot3(inverses[s], split2(info_ref[s, lo:hi, 128 * j : 128 * j + 128]), NN)
                out_ref[s, lo:hi, 128 * j : 128 * j + 128] = u
                right[j][s] = split2(u)
            for i in range(k + 1, j + 1):
                for s in range(slices):
                    less = dot3(right[i][s], right[j][s], TN)
                    info_ref[s, 128 * i : 128 * i + 128, 128 * j : 128 * j + 128] -= less
        copy = pltpu.make_async_copy(out_ref.at[:, lo:hi, :], out_hbm.at[:, lo:hi, :], out_sems.at[k])
        copy.start()
        leaving.append(copy)
    for copy in leaving:
        copy.wait()


def factor(arrived, prior_gram):
    slices, width, _ = prior_gram.shape
    hbm = pl.BlockSpec(memory_space=pltpu.HBM)
    return pl.pallas_call(
        factor_kernel,
        out_shape=jax.ShapeDtypeStruct(prior_gram.shape, F32),
        in_specs=[hbm, pl.BlockSpec(memory_space=pl.ANY)],
        out_specs=hbm,
        scratch_shapes=[
            pltpu.SMEM((3, 2 * arrived.shape[0] + 1), jnp.int32),
            pltpu.VMEM((arrived.shape[0], 8, 128), F32),
            pltpu.VMEM((arrived.shape[0] + 1, 3 * width, 128), F32),
            pltpu.VMEM((slices, width, width), F32),
            pltpu.VMEM((slices, width, width), F32),
            pltpu.VMEM((2, slices, 128, 128), F32),
            pltpu.SemaphoreType.DMA((arrived.shape[0],)),
            pltpu.SemaphoreType.DMA,
            pltpu.SemaphoreType.DMA,
            pltpu.SemaphoreType.DMA((width // 128,)),
        ],
        compiler_params=pltpu.CompilerParams(vmem_limit_bytes=VMEM_LIMIT),
    )(arrived, prior_gram)


def per_device(local_obs, global_obs, row_counts, owner_map, prior_factor):
    arc_dev = local_obs.shape[0]
    arc_groups = lax.axis_size("arc")
    col_groups = lax.axis_size("col")
    counts = lax.dynamic_slice_in_dim(row_counts, lax.axis_index("col") * arc_dev, arc_dev)
    packed = layout(jnp.transpose(global_obs, (1, 2, 0)))
    columns = lax.all_to_all(packed, "col", split_axis=0, concat_axis=0, tiled=True)
    columns = columns.reshape(col_groups, arc_dev, *packed.shape[1:])
    order = jnp.arange(arc_dev, dtype=jnp.int32)
    dest = owner_map // SLICE_DEV // col_groups
    earlier = (dest[None, :] == dest[:, None]) & (order[None, :] < order[:, None])
    slot = jnp.sum(earlier.astype(jnp.int32), axis=1)
    z, prior_gram = local_part(counts, local_obs, prior_factor)
    kept = eliminate(dest, slot, owner_map % SLICE_DEV, columns, z, arc_groups)
    arrived = lax.all_to_all(kept, "arc", split_axis=0, concat_axis=0, tiled=True)
    return factor(arrived, prior_gram)


def solution(mesh):
    placed = (
        P(("arc", "col"), None, None),
        P("arc", None, "col"),
        P("arc"),
        P(("arc", "col")),
        P(("arc", "col"), None, None),
    )
    return jax.shard_map(
        per_device,
        mesh=mesh,
        in_specs=placed,
        out_specs=P(("arc", "col"), None, None),
        check_vma=False,
    )
```
